32 devices in a mesh: shot: 2 (over x), sub: 16 (over z, y, core).
Axes of the slice: x: 2, y: 2, z: 4, core: 2. Of those that a mesh axis runs over, the one named last changes fastest.
Arguments:
- synthetic: float32 [16384, 256], P(('shot', 'sub')), parts along dimension 0, may hold values from -6 to 6
- observed: float32 [16384, 256], P(('shot', 'sub')), parts along dimension 0, may hold values from -6 to 6
- offsets: int32 [16384], P(('shot', 'sub')), parts along dimension 0, may hold values from 0 to 127
- lines: int32 [2, 16384], P(None, ('shot', 'sub')), parts along dimension 1, may hold values from 0 to 63, as said below
- owners: int32 [16384, 1], P(('shot', 'sub')), parts along dimension 0, may hold values from 0 to 15; in each aligned block of 512 rows (0 to 511, 512 to 1023, ...) at most 64 rows name the same one
- cells: int32 [16384], P(('shot', 'sub')), parts along dimension 0, may hold values from 0 to 65535
- taps: float32 [128], replicated, may hold values from -0.5 to 0.5
- line_taps: float32 [9], replicated, may hold values from -2 to 2
- velocity: float32 [128, 64, 128], P('sub'), may hold values from 1 to 2.5
- adjoint_old: float32 [256, 64, 128], P(('shot', 'sub')), parts along dimension 0, may hold values from -6 to 6
- adjoint_now: float32 [256, 64, 128], P(('shot', 'sub')), parts along dimension 0, may hold values from -6 to 6
- forward: float32 [4, 256, 64, 128], P(None, ('shot', 'sub')), parts along dimension 1, may hold values from -6 to 6
Outputs:
- adjoint_prior: float32 [256, 64, 128], P(('shot', 'sub')), parts along dimension 0
- adjoint_next: float32 [256, 64, 128], P(('shot', 'sub')), parts along dimension 0
- gradient: float32 [256, 64, 128], P(('shot', 'sub')), parts along dimension 0
The draws below stay inside these ranges and needn't reach their ends.
There are 2 independent parts, one for each index of `shot`. The reference program is written for one: setup_inputs(seed, part) draws one part's arguments, and reference() takes and returns one part's arrays. A program takes and returns all parts, laid end to end along the dimension named above; an argument that names none is the same for every part. Nothing has to cross between parts.
Inputs may be any that keep to these rules, and one draw needn't show every extreme that they name: `owners`: among the receivers of one device at most 64 have the same owner, and in some devices some owner has exactly 64. `lines`: row 0 counts the receivers before a receiver on its line, row 1 those after it; each line is a run of at most 64 consecutive receivers, and some line has exactly 64.
All inputs are finite; a program needn't handle non-finite values.
Results may differ from the reference program's by a relative error of at most 0.00017.
Values sent between devices are 32-bit elements; how exact they have to be, the bound alone decides.
No kernel may reach another device: no remote copies, remote signals or barrier semaphores. Data moves between devices by JAX's collectives and lax.ppermute only.
A program may use at most 128 MiB of HBM per device.

```python
import math
import jax
import jax.numpy as jnp
import numpy as np
from jax import lax

CX = 8
NY = 64
NZ = 128
RCV_DEV = 512
NT = 256
NTAP = 128
SW = 4
STEPS = 2
RCV = 8192
NX = 128
CAP = 64


def draw_lines(key, part):
    key = jax.random.fold_in(key, 7)
    phase_key = jax.random.fold_in(key, 1)
    start_key = jax.random.fold_in(key, 2)
    phase = 2 * jax.random.randint(phase_key, (), 2, 30) + 1
    position = jnp.arange(RCV, dtype=jnp.int32)
    local = position % RCV_DEV
    drawn = (local < 5) | (local >= RCV_DEV - 4) | (position < 128)
    random_starts = (jax.random.randint(start_key, (RCV,), 0, 16) == 0) & jnp.logical_not(drawn)
    starts = random_starts | ((position + phase) % 64 == 0) | (position == 0)
    first = lax.cummax(jnp.where(starts, position, 0), axis=0)
    later = jnp.concatenate([jnp.where(starts, position, RCV)[1:], jnp.full((1,), RCV, jnp.int32)])
    following = lax.cummin(later, axis=0, reverse=True)
    return jnp.stack([position - first, following - position - 1]).astype(jnp.int32)


def with_ends(result, rng, smallest, top_value):
    longest = result.shape.index(max(result.shape))
    spots = []
    for shift in (0, 1):
        where = [jax.random.randint(jax.random.fold_in(rng, axis), (), 0, length) for axis, length in enumerate(result.shape)]
        where[longest] = (where[longest] + shift) % result.shape[longest]
        spots.append(tuple(where))
    return result.at[spots[0]].set(smallest).at[spots[1]].set(top_value)


def level_of(rng, dims, shards, least, largest):
    def one(axis_at, parts):
        steps = jax.random.uniform(jax.random.fold_in(jax.random.fold_in(rng, 6), axis_at), (parts,), jnp.float32, least / len(shards), largest / len(shards))
        return jnp.repeat(jnp.exp(steps), dims[axis_at] // parts).reshape((-1,) + (1,) * (len(dims) - axis_at - 1))

    level = one(*shards[0])
    for cut in shards[1:]:
        level = level * one(*cut)
    return level


def shared_out(stream_key, own, number, rows, amount, top, most, skew):
    sequence = jax.random.permutation(stream_key, amount)
    crowded, common = portions_of(amount, rows * top, most, skew, True), portions_of(amount, rows * top, most, skew, False)
    places = jnp.arange(amount)

    def named(sizes, rotation):
        used = int((sizes > 0).sum())
        fixed = max(1, used // 4)
        moved = fixed + (places - fixed + rotation * (used - fixed)) % max(1, amount - fixed)
        return jnp.zeros((amount,), jnp.int32).at[sequence[jnp.where(places < fixed, places, moved)]].set(jnp.asarray(sizes, jnp.int32))

    sizes = jnp.where(number % 4 == 0, named(crowded, number // 4), named(common, number - number // 4 - 1))
    mixed = jax.random.permutation(jax.random.fold_in(own, 3), amount)
    giver, receiver = mixed[0:amount // 2 * 2:2], mixed[1:amount // 2 * 2:2]
    slack = jnp.minimum(sizes[giver] - 1, most - sizes[receiver]) // 2
    slack = jnp.where((giver == sequence[0]) | (receiver == sequence[0]) | (sizes[receiver] == 0), 0, jnp.maximum(slack, 0))
    moved = jax.random.randint(jax.random.fold_in(own, 4), (amount // 2,), 0, 1 << 20) % (slack + 1)
    sizes = sizes.at[giver].add(-moved).at[receiver].add(moved)
    labels = jnp.searchsorted(jnp.cumsum(sizes), jnp.arange(rows * top), side="right").astype(jnp.int32)
    table = labels.reshape(top, rows).T
    table = table[jax.random.permutation(jax.random.fold_in(own, 1), rows)]
    rotation = jax.random.randint(jax.random.fold_in(own, 2), (rows, 1), 0, top)
    return jnp.take_along_axis(table, (jnp.arange(top)[None, :] + rotation) % top, axis=1)


def portions_of(count, total, most, slope, full):
    portions = [(1 << 20) // math.isqrt(rank ** slope) + 1 for rank in range(1, count + 1)]
    largest = most if full else min(most, max(-(-total // count), total * portions[0] // sum(portions)))
    least = 1 if total - largest >= count - 1 else 0
    counts, rest = [largest] + [least] * (count - 1), total - largest - least * (count - 1)
    while rest > 0:
        candidates = [i for i in range(1, count) if counts[i] < largest] or [i for i in range(1, count) if counts[i] < most]
        whole, left = sum([portions[i] for i in candidates]), rest
        for i in candidates:
            addition = min(most - counts[i], max(1, left * portions[i] // whole), rest)
            counts[i] = counts[i] + addition
            rest = rest - addition
    return np.array(counts)


def gaussian(rng, shape, width, bound, cuts=(), kind=jnp.bfloat16):
    loudness = level_of(rng, shape, cuts, -0.22, 0.18) if cuts else 1.0
    array = jax.random.normal(rng, shape, jnp.float32) * width * loudness
    return jnp.minimum(jnp.maximum(array, -bound), bound).astype(kind)


def setup_inputs(seed: int = 0, part: int = 0) -> dict:
    arg_keys = jax.random.split(jax.random.key(seed), 13)
    part_keys = jax.random.split(jax.random.fold_in(arg_keys[12], part), 13)
    synthetic = gaussian(part_keys[0], (RCV, NT), 1.0, 6.0, ((0, 16),), jnp.float32)
    observed = gaussian(part_keys[1], (RCV, NT), 1.0, 6.0, ((0, 16),), jnp.float32)
    offsets = with_ends(jax.random.randint(part_keys[2], (RCV,), 0, NT - NTAP - STEPS + 2), jax.random.fold_in(part_keys[2], 1), 0, (NT - NTAP - STEPS + 2) - 1).astype(jnp.int32)
    lines = draw_lines(jax.random.fold_in(jax.random.fold_in(arg_keys[12], part), 71), part)
    owners_keys = jax.random.split(jax.random.fold_in(part_keys[4], 1), RCV // RCV_DEV)
    owners_turns = jax.random.permutation(jax.random.fold_in(part_keys[4], 3), RCV // RCV_DEV)
    owners = jax.vmap(lambda own, number: shared_out(jax.random.fold_in(part_keys[4], 2), own, number, RCV_DEV, NX // CX, 1, CAP, 2))(owners_keys, owners_turns).reshape((RCV, 1))
    cells = with_ends(jax.random.randint(part_keys[5], (RCV,), 0, CX * NY * NZ), jax.random.fold_in(part_keys[5], 1), 0, (CX * NY * NZ) - 1).astype(jnp.int32)
    taps = gaussian(arg_keys[6], (NTAP,), NTAP ** -0.5, 0.5, (), jnp.float32)
    line_taps = gaussian(arg_keys[7], (2 * SW + 1,), (2 * SW + 1) ** -0.5, 2.0, (), jnp.float32)
    velocity = jnp.clip(1.0 + 1.5 * jax.random.uniform(arg_keys[8], (NX, NY, NZ), jnp.float32) ** level_of(arg_keys[8], (NX, NY, NZ), ((0, 16),), -0.2, 0.2), 1.0, 2.5)
    adjoint_old = gaussian(part_keys[9], (NX, NY, NZ), 1.0, 6.0, ((0, 16),), jnp.float32)
    adjoint_now = gaussian(part_keys[10], (NX, NY, NZ), 1.0, 6.0, ((0, 16),), jnp.float32)
    forward = gaussian(part_keys[11], (STEPS + 2, NX, NY, NZ), 1.0, 6.0, ((1, 16),), jnp.float32)
    return {"synthetic": synthetic, "observed": observed, "offsets": offsets, "lines": lines, "owners": owners, "cells": cells, "taps": taps, "line_taps": line_taps, "velocity": velocity, "adjoint_old": adjoint_old, "adjoint_now": adjoint_now, "forward": forward}


COEF = (-205.0 / 72.0, 8.0 / 5.0, -1.0 / 5.0, 8.0 / 315.0, -1.0 / 560.0)
DT_OVER_H = 0.18


def laplacian(field):
    padded = jnp.pad(field, 4)
    size_x, size_y, size_z = field.shape
    total = (3.0 * COEF[0]) * field
    for order in range(1, 5):
        total = total + COEF[order] * (
            padded[4 + order:4 + order + size_x, 4:4 + size_y, 4:4 + size_z]
            + padded[4 - order:4 - order + size_x, 4:4 + size_y, 4:4 + size_z]
            + padded[4:4 + size_x, 4 + order:4 + order + size_y, 4:4 + size_z]
            + padded[4:4 + size_x, 4 - order:4 - order + size_y, 4:4 + size_z]
            + padded[4:4 + size_x, 4:4 + size_y, 4 + order:4 + order + size_z]
            + padded[4:4 + size_x, 4:4 + size_y, 4 - order:4 - order + size_z])
    return total


def cut_window(trace, start):
    return lax.dynamic_slice_in_dim(trace, start, NTAP + STEPS - 1)


def time_filter(window, taps):
    columns = [jnp.dot(window[:, lag:lag + NTAP], taps, precision=lax.Precision.HIGHEST) for lag in range(STEPS)]
    return jnp.stack(columns, axis=1)


def line_filter(wide, lines, line_taps, count):
    before = lines[0]
    after = lines[1]
    total = jnp.zeros((count, wide.shape[1]), jnp.float32)
    for reach in range(-SW, SW + 1):
        neighbour = wide[SW + reach:SW + reach + count]
        if reach < 0:
            keep = before >= -reach
        elif reach > 0:
            keep = after >= reach
        else:
            keep = before >= 0
        total = total + jnp.where(keep[:, None], line_taps[reach + SW] * neighbour, 0.0)
    return total


def reference(synthetic, observed, offsets, lines, owners, cells, taps, line_taps, velocity, adjoint_old, adjoint_now, forward):
    residual = synthetic - observed
    window = jax.vmap(cut_window)(residual, offsets)
    filtered = time_filter(window, taps)
    wide = jnp.pad(filtered, ((SW, SW), (0, 0)))
    sources = line_filter(wide, lines, line_taps, RCV)
    block = CX * NY * NZ
    target = owners[:, 0] * block + cells
    flat = jnp.zeros((STEPS, NX * NY * NZ), jnp.float32).at[:, target].add(sources.T)
    injected = flat.reshape(STEPS, NX, NY, NZ)
    scale = (DT_OVER_H * velocity) ** 2
    weight = 2.0 / (velocity * velocity * velocity)
    gradient = jnp.zeros_like(velocity)
    older, newer = adjoint_old, adjoint_now
    for step in range(STEPS):
        fresh = 2.0 * newer - older + scale * (laplacian(newer) + injected[step])
        gradient = gradient + weight * fresh * (forward[step] - 2.0 * forward[step + 1] + forward[step + 2])
        older, newer = newer, fresh
    return older, newer, gradient
```

```python
import functools

import jax
import jax.numpy as jnp
from jax import lax
from jax.experimental import pallas as pl
from jax.experimental.pallas import tpu as pltpu
from jax.sharding import PartitionSpec as P

SW = 4
STEPS = 2
REACH = 4
LANES = 128
EDGE = 2 * SW

COEF = (-205.0 / 72.0, 8.0 / 5.0, -1.0 / 5.0, 8.0 / 315.0, -1.0 / 560.0)
DT_OVER_H = 0.18

VMEM = pl.BlockSpec(memory_space=pltpu.VMEM)
SMEM = pl.BlockSpec(memory_space=pltpu.SMEM)
NT_DIMS = (((1,), (1,)), ((), ()))


def parts_of(value, count):
    parts = []
    for _ in range(count):
        part = value.astype(jnp.bfloat16).astype(jnp.float32)
        parts.append(part)
        value = value - part
    return parts


def iota(shape, axis):
    return lax.broadcasted_iota(jnp.int32, shape, axis)


def pack_kernel(
    devices, cap, block, syn, obs, off, lines, own, cells, taps, line_taps, send
):
    me = lax.axis_index("sub")
    count, samples = syn.shape
    ntap = taps.shape[1]
    residual = syn[...] - obs[...]
    starts = -(-(samples - ntap + 1) // 8) * 8
    row = jnp.concatenate([taps[...], jnp.zeros((1, samples - ntap), jnp.float32)], axis=1)
    toeplitz = pltpu.roll(
        jnp.broadcast_to(row, (starts, samples)), 0, 1, stride=1, stride_axis=0
    )
    all_starts = lax.dot_general(
        toeplitz,
        residual,
        NT_DIMS,
        precision=lax.Precision.HIGHEST,
        preferred_element_type=jnp.float32,
    )
    start = iota((starts, count), 0)
    offset = off[...]
    filtered = [
        jnp.sum(jnp.where(start == offset + step, all_starts, 0.0), axis=0, keepdims=True)
        for step in range(STEPS)
    ]
    both = jnp.concatenate(filtered + [jnp.zeros((8 - STEPS, count), jnp.float32)], axis=0)
    place = iota((1, count), 1)
    before = lines[0:1, :]
    after = lines[1:2, :]
    sources = jnp.zeros((8, count), jnp.float32)
    for reach in range(-SW, SW + 1):
        term = line_taps[reach + SW] * (
            pltpu.roll(both, (-reach) % count, 1) if reach else both
        )
        if reach < 0:
            keep = (before >= -reach) & (place >= -reach)
        elif reach > 0:
            keep = (after >= reach) & (place < count - reach)
        else:
            keep = before >= 0
        sources = sources + jnp.where(keep, term, 0.0)
    owner = own[...]
    hot = iota((devices, count), 0) == owner
    hot_f = hot.astype(jnp.float32)
    earlier = (iota((count, count), 0) < iota((count, count), 1)).astype(jnp.float32)
    ranks = jnp.dot(
        hot_f.astype(jnp.bfloat16),
        earlier.astype(jnp.bfloat16),
        preferred_element_type=jnp.float32,
    )
    rank = jnp.sum(jnp.where(hot, ranks, 0.0), axis=0, keepdims=True).astype(jnp.int32)
    cell = cells[...]
    high = (cell >> 8).astype(jnp.float32)
    low = (cell & 255).astype(jnp.float32)
    pieces = parts_of(sources[0:1], 3) + parts_of(sources[1:2], 3) + [high, low]
    spread = jnp.concatenate([hot_f * piece for piece in pieces], axis=0).astype(jnp.bfloat16)
    pack = LANES // cap
    lane = iota((LANES, count), 0)
    slot = (lane == rank + (me % pack) * cap).astype(jnp.float32).astype(jnp.bfloat16)
    out = lax.dot_general(spread, slot, NT_DIMS, preferred_element_type=jnp.float32)
    part = [out[k * devices : (k + 1) * devices] for k in range(8)]
    value0 = part[0] + part[1] + part[2]
    value1 = part[3] + part[4] + part[5]
    where = 256.0 * part[6] + part[7]
    none = jnp.zeros((1, LANES), jnp.float32)

    def to_upper(rows):
        return pltpu.roll(jnp.concatenate([none, rows[:-1]], axis=0), LANES // 2, 1)

    def to_lower(rows):
        return pltpu.roll(jnp.concatenate([rows[1:], none], axis=0), LANES // 2, 1)

    send[:, 0, :] = value0 + to_upper(value0)
    send[:, 1, :] = where + to_upper(where)
    send[:, 2, :] = value1 + to_lower(value0)
    send[:, 3, :] = to_lower(where)
    group = LANES // EDGE
    count_ = jnp.where(place < SW, before, after).astype(jnp.float32)
    edge_rows = (
        parts_of(both[0:1], 3)
        + parts_of(both[1:2], 3)
        + [owner.astype(jnp.float32), high, low, count_]
    )
    edge_rows = jnp.concatenate(
        edge_rows + [jnp.zeros((16 - len(edge_rows), count), jnp.float32)], axis=0
    ).astype(jnp.bfloat16)
    edge_lane = jnp.where(
        place < SW, place, jnp.where(place >= count - SW, place - count + EDGE, -LANES)
    )
    chosen = (lane == edge_lane + (me % group) * EDGE).astype(jnp.float32).astype(jnp.bfloat16)
    edge = lax.dot_general(edge_rows, chosen, NT_DIMS, preferred_element_type=jnp.float32)
    edge_cell = edge[6:7] * float(block) + 256.0 * edge[7:8] + edge[8:9]
    shape = (devices, LANES)
    send[:, 4, :] = jnp.broadcast_to(edge[0:1] + edge[1:2] + edge[2:3], shape)
    send[:, 5, :] = jnp.broadcast_to(edge[3:4] + edge[4:5] + edge[5:6], shape)
    send[:, 6, :] = jnp.broadcast_to(edge_cell, shape)
    send[:, 7, :] = jnp.broadcast_to(edge[9:10], shape)


PAD = 8


def laplacian_plane(field, x, size_y):
    centre = field[x, PAD : PAD + size_y, :]
    lanes = centre.shape[1]
    lane = iota(centre.shape, 1)
    total = 3.0 * COEF[0] * centre
    for k in range(1, 5):
        near = field[x + k, PAD : PAD + size_y, :] + field[x - k, PAD : PAD + size_y, :]
        near = near + field[x, PAD + k : PAD + k + size_y, :]
        near = near + field[x, PAD - k : PAD - k + size_y, :]
        near = near + jnp.where(lane < lanes - k, pltpu.roll(centre, lanes - k, 1), 0.0)
        near = near + jnp.where(lane >= k, pltpu.roll(centre, k, 1), 0.0)
        total = total + COEF[k] * near
    return total


def first_kernel(
    from_pair, from_next, old, now, vel, fwd, free, scale, weight0, weight1, wide, edges
):
    odd = lax.axis_index("sub") % 2
    size_x, size_y, lanes = old.shape
    zeros = jnp.zeros((wide.shape[0], PAD, lanes), jnp.float32)
    wide[:, 0:PAD, :] = zeros
    wide[:, PAD + size_y :, :] = zeros
    inside = slice(PAD, PAD + size_y)
    wide[2 * REACH : 2 * REACH + size_x, inside, :] = now[...]
    above = 2 * REACH + size_x

    def place(lower, upper):
        wide[0 : 2 * REACH, inside, :] = lower[0 : 2 * REACH]
        wide[above : above + 2 * REACH, inside, :] = upper[0 : 2 * REACH]
        edges[0] = lower[2 * REACH : 3 * REACH]
        edges[1] = lower[3 * REACH : 4 * REACH]
        edges[2] = upper[2 * REACH : 3 * REACH]
        edges[3] = upper[3 * REACH : 4 * REACH]

    @pl.when(odd == 0)
    def _():
        place(from_next, from_pair)

    @pl.when(odd == 1)
    def _():
        place(from_pair, from_next)

    def step(out_x, older, speed):
        factor = DT_OVER_H * speed
        factor = factor * factor
        scale[out_x] = factor
        x = out_x + REACH
        free[out_x] = (
            2.0 * wide[x, inside, :] - older + factor * laplacian_plane(wide, x, size_y)
        )

    @pl.loop(0, REACH)
    def _(x):
        step(x, edges[0, x], edges[1, x])
        step(x + REACH + size_x, edges[2, x], edges[3, x])

    @pl.loop(0, size_x)
    def _(x):
        speed = vel[x]
        step(x + REACH, old[x], speed)
        weight = 2.0 / (speed * speed * speed)
        f1 = fwd[1, x]
        f2 = fwd[2, x]
        weight0[x] = weight * (fwd[0, x] - 2.0 * f1 + f2)
        weight1[x] = weight * (f1 - 2.0 * f2 + fwd[3, x])


def second_kernel(
    devices,
    cap,
    got,
    line_taps,
    free,
    scale,
    now,
    weight0,
    weight1,
    prior,
    last,
    gradient,
    field,
    source1,
):
    me = lax.axis_index("sub")
    size_x, size_y, lanes = now.shape
    rows = size_x * size_y
    halo = REACH * size_y
    block = rows * lanes
    pack = LANES // cap
    lane8 = iota((8, LANES), 1)

    group = LANES // EDGE
    edge_parts = []
    for g in range(-(-devices // group)):
        total = got[g * group]
        for i in range(g * group + 1, min(devices, (g + 1) * group)):
            total = total + got[i]
        edge_parts.append(total)
    edge = jnp.concatenate(edge_parts, axis=1)
    width = edge.shape[1]
    spot = iota((8, width), 1)
    e = spot % EDGE
    count = edge[7:8]
    missing = jnp.zeros((8, width), jnp.float32)
    for reach in range(-SW, SW + 1):
        if reach == 0:
            continue
        if reach < 0:
            crosses = (e < -reach) & (spot >= -reach)
        else:
            crosses = (e >= EDGE - reach) & (spot < width - reach)
        keep = crosses & (count >= float(abs(reach)))
        missing = missing + jnp.where(
            keep, line_taps[reach + SW] * pltpu.roll(edge, (-reach) % width, 1), 0.0
        )
    edge_cell = edge[6:7].astype(jnp.int32) - me * block

    zs = iota((LANES, LANES), 0)
    row_own = iota((rows, LANES), 0)
    row_halo = iota((halo, LANES), 0)

    def hot_rows(cell, shift, index):
        at = (cell >> (lanes.bit_length() - 1)) + shift
        return (index == at).astype(jnp.float32).astype(jnp.bfloat16)

    def spread(cell, values):
        hot = zs == (cell & (lanes - 1))
        stack = []
        for value in values:
            for part in parts_of(value, 2):
                stack.append(jnp.where(hot, part, 0.0))
        return jnp.concatenate(stack, axis=0).astype(jnp.bfloat16)

    own_a, own_b, low_a, low_b, high_a, high_b = [], [], [], [], [], []

    for g in range(devices // pack):
        tiles = [got[g * pack + q] for q in range(pack)]
        mine, other = tiles[0], tiles[pack // 2]
        for q in range(1, pack):
            later = lane8 >= q * cap
            mine = jnp.where(later, tiles[q], mine)
            other = jnp.where(later, tiles[(q + pack // 2) % pack], other)
        cell = mine[1:2].astype(jnp.int32)
        own_a.append(hot_rows(cell, 0, row_own))
        own_b.append(spread(cell, [mine[0:1], mine[2:3]]))
        cell = other[1:2].astype(jnp.int32)
        low_a.append(hot_rows(cell, halo - rows, row_halo))
        low_b.append(spread(cell, [other[0:1]]))
        cell = other[3:4].astype(jnp.int32)
        high_a.append(hot_rows(cell, 0, row_halo))
        high_b.append(spread(cell, [other[2:3]]))
    for g in range(width // LANES):
        at = slice(g * LANES, (g + 1) * LANES)
        cell = edge_cell[:, at]
        b = spread(cell, [missing[4:5, at], missing[5:6, at]])
        own_a.append(hot_rows(cell, 0, row_own))
        own_b.append(b)
        low_a.append(hot_rows(cell, halo, row_halo))
        low_b.append(b[: 2 * LANES])
        high_a.append(hot_rows(cell, -rows, row_halo))
        high_b.append(b[: 2 * LANES])

    def inject(a, b):
        return lax.dot_general(
            jnp.concatenate(a, axis=1),
            jnp.concatenate(b, axis=1),
            NT_DIMS,
            preferred_element_type=jnp.float32,
        )

    zeros = jnp.zeros((field.shape[0], PAD, lanes), jnp.float32)
    field[:, 0:PAD, :] = zeros
    field[:, PAD + size_y :, :] = zeros
    inside = slice(PAD, PAD + size_y)
    top = REACH + size_x

    out = inject(own_a, own_b)
    first = (out[:, 0:lanes] + out[:, lanes : 2 * lanes]).reshape(size_x, size_y, lanes)
    source1[...] = (out[:, 2 * lanes : 3 * lanes] + out[:, 3 * lanes :]).reshape(
        size_x, size_y, lanes
    )
    fresh = free[REACH:top] + scale[REACH:top] * first
    prior[...] = fresh
    field[REACH:top, inside, :] = fresh
    out = inject(low_a, low_b)
    first = (out[:, 0:lanes] + out[:, lanes:]).reshape(REACH, size_y, lanes)
    field[0:REACH, inside, :] = free[0:REACH] + scale[0:REACH] * first
    out = inject(high_a, high_b)
    first = (out[:, 0:lanes] + out[:, lanes:]).reshape(REACH, size_y, lanes)
    field[top:, inside, :] = free[top:] + scale[top:] * first

    @pl.loop(0, size_x)
    def _(x):
        at = x + REACH
        fresh = field[at, inside, :]
        following = (
            2.0 * fresh
            - now[x]
            + scale[at] * (laplacian_plane(field, at, size_y) + source1[x])
        )
        last[x] = following
        gradient[x] = weight0[x] * fresh + weight1[x] * following


def body(
    synthetic,
    observed,
    offsets,
    lines,
    owners,
    cells,
    taps,
    line_taps,
    velocity,
    adjoint_old,
    adjoint_now,
    forward,
):
    count = synthetic.shape[0]
    size_x, size_y, lanes = velocity.shape
    devices = lax.axis_size("sub")
    me = lax.axis_index("sub")
    cap = max(2, 2 * count // devices)
    f32 = jnp.float32

    pair = [(i, i ^ 1) for i in range(devices)]
    following = [(i, i + 1) for i in range(1, devices - 1, 2)]
    following = following + [(b, a) for a, b in following]

    def edge_planes(start):
        return jnp.concatenate(
            [
                adjoint_now,
                lax.dynamic_slice_in_dim(adjoint_old, start, REACH, 0),
                lax.dynamic_slice_in_dim(velocity, start, REACH, 0),
            ],
            axis=0,
        )

    odd = me % 2
    top = size_x - REACH
    from_pair = lax.ppermute(edge_planes(jnp.where(odd == 0, top, 0)), "sub", pair)
    from_next = lax.ppermute(edge_planes(jnp.where(odd == 0, 0, top)), "sub", following)

    send = pl.pallas_call(
        functools.partial(pack_kernel, devices, cap, velocity.size),
        out_shape=jax.ShapeDtypeStruct((devices, 8, LANES), f32),
        in_specs=[VMEM] * 7 + [SMEM],
        out_specs=VMEM,
        name="pack",
    )(
        synthetic,
        observed,
        offsets.reshape(1, count),
        lines,
        owners.reshape(1, count),
        cells.reshape(1, count),
        taps.reshape(1, -1),
        line_taps,
    )
    got = lax.all_to_all(send, "sub", split_axis=0, concat_axis=0, tiled=True)

    plane = (size_y, lanes)
    outer = size_x + 2 * REACH
    free, scale, weight0, weight1 = pl.pallas_call(
        first_kernel,
        out_shape=(
            jax.ShapeDtypeStruct((outer,) + plane, f32),
            jax.ShapeDtypeStruct((outer,) + plane, f32),
            jax.ShapeDtypeStruct((size_x,) + plane, f32),
            jax.ShapeDtypeStruct((size_x,) + plane, f32),
        ),
        in_specs=[VMEM] * 6,
        out_specs=(VMEM,) * 4,
        scratch_shapes=[
            pltpu.VMEM((size_x + 4 * REACH, size_y + 2 * PAD, lanes), f32),
            pltpu.VMEM((4, REACH) + plane, f32),
        ],
        name="first",
    )(from_pair, from_next, adjoint_old, adjoint_now, velocity, forward)

    field = jax.ShapeDtypeStruct((size_x,) + plane, f32)
    return pl.pallas_call(
        functools.partial(second_kernel, devices, cap),
        out_shape=(field, field, field),
        in_specs=[VMEM, SMEM] + [VMEM] * 5,
        out_specs=(VMEM,) * 3,
        scratch_shapes=[
            pltpu.VMEM((outer, size_y + 2 * PAD, lanes), f32),
            pltpu.VMEM((size_x,) + plane, f32),
        ],
        name="second",
    )(got, line_taps, free, scale, adjoint_now, weight0, weight1)


def solution(mesh):
    return jax.shard_map(
        body,
        mesh=mesh,
        in_specs=(
            P(("shot", "sub"), None),
            P(("shot", "sub"), None),
            P(("shot", "sub")),
            P(None, ("shot", "sub")),
            P(("shot", "sub"), None),
            P(("shot", "sub")),
            P(),
            P(),
            P("sub", None, None),
            P(("shot", "sub"), None, None),
            P(("shot", "sub"), None, None),
            P(None, ("shot", "sub"), None, None),
        ),
        out_specs=(
            P(("shot", "sub"), None, None),
            P(("shot", "sub"), None, None),
            P(("shot", "sub"), None, None),
        ),
        check_vma=False,
    )
```

```python
import functools

import jax
import jax.numpy as jnp
from jax import lax
from jax.experimental import pallas as pl
from jax.experimental.pallas import tpu as pltpu
from jax.sharding import PartitionSpec as P

SW = 4
STEPS = 2
REACH = 4
LANES = 128
EDGE = 2 * SW

COEF = (-205.0 / 72.0, 8.0 / 5.0, -1.0 / 5.0, 8.0 / 315.0, -1.0 / 560.0)
DT_OVER_H = 0.18

VMEM = pl.BlockSpec(memory_space=pltpu.VMEM)
FAR = pl.BlockSpec(memory_space=pltpu.HBM)
PARAMS = pltpu.CompilerParams(vmem_limit_bytes=16 * 2**20)
NT_DIMS = (((1,), (1,)), ((), ()))


def near(array):
    return pltpu.with_memory_space_constraint(array, pltpu.VMEM)


def far(*arrays):
    return [pltpu.with_memory_space_constraint(array, pltpu.HBM) for array in arrays]


def started(sems, *pairs):
    copies = [
        pltpu.make_async_copy(source, target, sems.at[i])
        for i, (source, target) in enumerate(pairs)
    ]
    for copy in copies:
        copy.start()
    return copies


def parts_of(value, count):
    parts = []
    for _ in range(count):
        part = value.astype(jnp.bfloat16).astype(jnp.float32)
        parts.append(part)
        value = value - part
    return parts


def iota(shape, axis):
    return lax.broadcasted_iota(jnp.int32, shape, axis)


PAD = 8


def laplacian_plane(field, x, size_y):
    centre = field[x, PAD : PAD + size_y, :]
    lanes = centre.shape[1]
    lane = iota(centre.shape, 1)
    total = 3.0 * COEF[0] * centre
    for k in range(1, 5):
        near = field[x + k, PAD : PAD + size_y, :] + field[x - k, PAD : PAD + size_y, :]
        near = near + field[x, PAD + k : PAD + k + size_y, :]
        near = near + field[x, PAD - k : PAD - k + size_y, :]
        near = near + jnp.where(lane < lanes - k, pltpu.roll(centre, lanes - k, 1), 0.0)
        near = near + jnp.where(lane >= k, pltpu.roll(centre, k, 1), 0.0)
        total = total + COEF[k] * near
    return total


def own_kernel(names, *refs):
    old_far, now_far, vel_far = refs[:3]
    sources = refs[3 : 3 + names]
    to_pair, to_next = refs[3 + names : 5 + names]
    targets = refs[5 + names : 5 + 2 * names]
    old, now, vel, wide, partial, sems = refs[5 + 2 * names :]
    odd = lax.axis_index("sub") % 2
    size_x, size_y, lanes = old.shape
    inside = slice(PAD, PAD + size_y)
    middle = wide.at[REACH : REACH + size_x, inside, :]
    copies = started(
        sems,
        (now_far, middle),
        (vel_far, vel),
        (old_far, old),
        *zip(sources, targets, strict=True),
    )
    planes = wide.shape[0]
    edge = jnp.zeros((planes, PAD, lanes), jnp.float32)
    wide[:, 0:PAD, :] = edge
    wide[:, PAD + size_y :, :] = edge
    blank = jnp.zeros((REACH, size_y, lanes), jnp.float32)
    wide[0:REACH, inside, :] = blank
    wide[REACH + size_x :, inside, :] = blank
    for copy in copies[:3]:
        copy.wait()

    def half(target, start):
        @pl.loop(0, REACH)
        def _(i):
            x = start + i
            own_now = wide[REACH + x, inside, :]
            speed = vel[x]
            factor = DT_OVER_H * speed
            target[i] = own_now
            target[REACH + i] = (
                2.0 * own_now
                - old[x]
                + factor * factor * laplacian_plane(wide, x + REACH, size_y)
            )
            target[2 * REACH + i] = speed

    far = size_x - REACH
    half(to_next, far * odd)
    half(to_pair, far * (1 - odd))
    for copy in copies[3:]:
        copy.wait()


def pack_kernel(
    devices,
    cap,
    block,
    line_taps_far,
    syn,
    obs,
    off,
    lines,
    own,
    cells,
    taps,
    send,
    line_taps,
    sems,
):
    copies = started(sems, (line_taps_far, line_taps))
    me = lax.axis_index("sub")
    count, samples = syn.shape
    ntap = taps.shape[1]
    residual = syn[...] - obs[...]
    starts = -(-(samples - ntap + 1) // 8) * 8
    row = jnp.concatenate([taps[...], jnp.zeros((1, samples - ntap), jnp.float32)], axis=1)
    toeplitz = pltpu.roll(
        jnp.broadcast_to(row, (starts, samples)), 0, 1, stride=1, stride_axis=0
    )
    all_starts = lax.dot_general(
        toeplitz,
        residual,
        NT_DIMS,
        precision=lax.Precision.HIGHEST,
        preferred_element_type=jnp.float32,
    )
    start = iota((starts, count), 0)
    offset = off[...]
    filtered = [
        jnp.sum(jnp.where(start == offset + step, all_starts, 0.0), axis=0, keepdims=True)
        for step in range(STEPS)
    ]
    both = jnp.concatenate(filtered + [jnp.zeros((8 - STEPS, count), jnp.float32)], axis=0)
    place = iota((1, count), 1)
    before = lines[0:1, :]
    after = lines[1:2, :]
    sources = jnp.zeros((8, count), jnp.float32)
    copies[0].wait()
    for reach in range(-SW, SW + 1):
        term = line_taps[reach + SW] * (
            pltpu.roll(both, (-reach) % count, 1) if reach else both
        )
        if reach < 0:
            keep = (before >= -reach) & (place >= -reach)
        elif reach > 0:
            keep = (after >= reach) & (place < count - reach)
        else:
            keep = before >= 0
        sources = sources + jnp.where(keep, term, 0.0)
    owner = own[...]
    hot = iota((devices, count), 0) == owner
    hot_f = hot.astype(jnp.float32)
    earlier = (iota((count, count), 0) < iota((count, count), 1)).astype(jnp.float32)
    ranks = jnp.dot(
        hot_f.astype(jnp.bfloat16),
        earlier.astype(jnp.bfloat16),
        preferred_element_type=jnp.float32,
    )
    rank = jnp.sum(jnp.where(hot, ranks, 0.0), axis=0, keepdims=True).astype(jnp.int32)
    cell = cells[...]
    high = (cell >> 8).astype(jnp.float32)
    low = (cell & 255).astype(jnp.float32)
    pieces = parts_of(sources[0:1], 3) + parts_of(sources[1:2], 3) + [high, low]
    spread = jnp.concatenate([hot_f * piece for piece in pieces], axis=0).astype(jnp.bfloat16)
    pack = LANES // cap
    lane = iota((LANES, count), 0)
    slot = (lane == rank + (me % pack) * cap).astype(jnp.float32).astype(jnp.bfloat16)
    out = lax.dot_general(spread, slot, NT_DIMS, preferred_element_type=jnp.float32)
    part = [out[k * devices : (k + 1) * devices] for k in range(8)]
    value0 = part[0] + part[1] + part[2]
    value1 = part[3] + part[4] + part[5]
    where = 256.0 * part[6] + part[7]
    none = jnp.zeros((1, LANES), jnp.float32)

    def to_upper(rows):
        return pltpu.roll(jnp.concatenate([none, rows[:-1]], axis=0), LANES // 2, 1)

    def to_lower(rows):
        return pltpu.roll(jnp.concatenate([rows[1:], none], axis=0), LANES // 2, 1)

    send[:, 0, :] = value0 + to_upper(value0)
    send[:, 1, :] = where + to_upper(where)
    send[:, 2, :] = value1 + to_lower(value0)
    send[:, 3, :] = to_lower(where)
    group = LANES // EDGE
    count_ = jnp.where(place < SW, before, after).astype(jnp.float32)
    edge_rows = (
        parts_of(both[0:1], 3)
        + parts_of(both[1:2], 3)
        + [owner.astype(jnp.float32), high, low, count_]
    )
    edge_rows = jnp.concatenate(
        edge_rows + [jnp.zeros((16 - len(edge_rows), count), jnp.float32)], axis=0
    ).astype(jnp.bfloat16)
    edge_lane = jnp.where(
        place < SW, place, jnp.where(place >= count - SW, place - count + EDGE, -LANES)
    )
    chosen = (lane == edge_lane + (me % group) * EDGE).astype(jnp.float32).astype(jnp.bfloat16)
    edge = lax.dot_general(edge_rows, chosen, NT_DIMS, preferred_element_type=jnp.float32)
    edge_cell = edge[6:7] * float(block) + 256.0 * edge[7:8] + edge[8:9]
    shape = (devices, LANES)
    send[:, 4, :] = jnp.broadcast_to(edge[0:1] + edge[1:2] + edge[2:3], shape)
    send[:, 5, :] = jnp.broadcast_to(edge[3:4] + edge[4:5] + edge[5:6], shape)
    send[:, 6, :] = jnp.broadcast_to(edge_cell, shape)
    send[:, 7, :] = jnp.broadcast_to(edge[9:10], shape)


def squared(speed):
    factor = DT_OVER_H * speed
    return factor * factor


def inner_kernel(old_far, now_far, vel_far, fwd_far, partial, weight0, weight1, wide, old, vel, fwd, sems):
    size_x, size_y, lanes = old.shape
    inside = slice(PAD, PAD + size_y)
    copies = started(
        sems,
        (now_far, wide.at[REACH : REACH + size_x, inside, :]),
        (vel_far, vel),
        (old_far, old),
        (fwd_far, fwd),
    )
    edge = jnp.zeros((wide.shape[0], PAD, lanes), jnp.float32)
    wide[:, 0:PAD, :] = edge
    wide[:, PAD + size_y :, :] = edge
    blank = jnp.zeros((REACH, size_y, lanes), jnp.float32)
    wide[0:REACH, inside, :] = blank
    wide[REACH + size_x :, inside, :] = blank
    for copy in copies:
        copy.wait()

    @pl.loop(0, size_x)
    def _(x):
        speed = vel[x]
        partial[x] = (
            2.0 * wide[REACH + x, inside, :]
            - old[x]
            + squared(speed) * laplacian_plane(wide, x + REACH, size_y)
        )
        weight = 2.0 / (speed * speed * speed)
        f1 = fwd[1, x]
        f2 = fwd[2, x]
        weight0[x] = weight * (fwd[0, x] - 2.0 * f1 + f2)
        weight1[x] = weight * (f1 - 2.0 * f2 + fwd[3, x])


def across(field, x, low, high):
    total = None
    for k in range(1, 5):
        for at in (x - k, x + k):
            if low <= at < high:
                term = COEF[k] * field[at - low]
                total = term if total is None else total + term
    return total


def first_kernel(
    from_pair, from_next, partial, now, vel, free, scale
):
    odd = lax.axis_index("sub") % 2
    size_x = now.shape[0]
    top = REACH + size_x

    def border(source, first_out, low):
        for i in range(REACH):
            factor = squared(source[2 * REACH + i])
            scale[first_out + i] = factor
            free[first_out + i] = source[REACH + i] + factor * across(now, low + i, 0, size_x)
        planes = range(REACH) if low < 0 else range(size_x - REACH, size_x)
        for x in planes:
            factor = squared(vel[x])
            scale[REACH + x] = factor
            free[REACH + x] = partial[x] + factor * across(source, x, low, low + REACH)

    @pl.when(odd == 0)
    def _():
        border(from_next, 0, -REACH)
        border(from_pair, top, size_x)

    @pl.when(odd == 1)
    def _():
        border(from_pair, 0, -REACH)
        border(from_next, top, size_x)


def second_kernel(
    devices,
    cap,
    got,
    line_taps_far,
    free_far,
    scale_far,
    now_far,
    weight0_far,
    weight1_far,
    prior_far,
    last_far,
    gradient_far,
    line_taps,
    free,
    scale,
    now,
    weight0,
    weight1,
    last,
    gradient,
    field,
    source1,
    sems,
    out_sems,
):
    copies = started(
        sems,
        (line_taps_far, line_taps),
        (free_far, free),
        (scale_far, scale),
        (now_far, now),
        (weight0_far, weight0),
        (weight1_far, weight1),
    )
    me = lax.axis_index("sub")
    size_x, size_y, lanes = now.shape
    rows = size_x * size_y
    halo = REACH * size_y
    block = rows * lanes
    pack = LANES // cap
    lane8 = iota((8, LANES), 1)

    group = LANES // EDGE
    edge_parts = []
    for g in range(-(-devices // group)):
        total = got[g * group]
        for i in range(g * group + 1, min(devices, (g + 1) * group)):
            total = total + got[i]
        edge_parts.append(total)
    edge = jnp.concatenate(edge_parts, axis=1)
    width = edge.shape[1]
    spot = iota((8, width), 1)
    e = spot % EDGE
    count = edge[7:8]
    missing = jnp.zeros((8, width), jnp.float32)
    copies[0].wait()
    for reach in range(-SW, SW + 1):
        if reach == 0:
            continue
        if reach < 0:
            crosses = (e < -reach) & (spot >= -reach)
        else:
            crosses = (e >= EDGE - reach) & (spot < width - reach)
        keep = crosses & (count >= float(abs(reach)))
        missing = missing + jnp.where(
            keep, line_taps[reach + SW] * pltpu.roll(edge, (-reach) % width, 1), 0.0
        )
    edge_cell = edge[6:7].astype(jnp.int32) - me * block

    zs = iota((LANES, LANES), 0)
    row_own = iota((rows, LANES), 0)
    row_halo = iota((halo, LANES), 0)

    def hot_rows(cell, shift, index):
        at = (cell >> (lanes.bit_length() - 1)) + shift
        return (index == at).astype(jnp.float32).astype(jnp.bfloat16)

    def spread(cell, values):
        hot = zs == (cell & (lanes - 1))
        stack = []
        for value in values:
            for part in parts_of(value, 2):
                stack.append(jnp.where(hot, part, 0.0))
        return jnp.concatenate(stack, axis=0).astype(jnp.bfloat16)

    own_a, own_b, low_a, low_b, high_a, high_b = [], [], [], [], [], []

    for g in range(devices // pack):
        tiles = [got[g * pack + q] for q in range(pack)]
        mine, other = tiles[0], tiles[pack // 2]
        for q in range(1, pack):
            later = lane8 >= q * cap
            mine = jnp.where(later, tiles[q], mine)
            other = jnp.where(later, tiles[(q + pack // 2) % pack], other)
        cell = mine[1:2].astype(jnp.int32)
        own_a.append(hot_rows(cell, 0, row_own))
        own_b.append(spread(cell, [mine[0:1], mine[2:3]]))
        cell = other[1:2].astype(jnp.int32)
        low_a.append(hot_rows(cell, halo - rows, row_halo))
        low_b.append(spread(cell, [other[0:1]]))
        cell = other[3:4].astype(jnp.int32)
        high_a.append(hot_rows(cell, 0, row_halo))
        high_b.append(spread(cell, [other[2:3]]))
    for g in range(width // LANES):
        at = slice(g * LANES, (g + 1) * LANES)
        cell = edge_cell[:, at]
        b = spread(cell, [missing[4:5, at], missing[5:6, at]])
        own_a.append(hot_rows(cell, 0, row_own))
        own_b.append(b)
        low_a.append(hot_rows(cell, halo, row_halo))
        low_b.append(b[: 2 * LANES])
        high_a.append(hot_rows(cell, -rows, row_halo))
        high_b.append(b[: 2 * LANES])

    def inject(a, b):
        return lax.dot_general(
            jnp.concatenate(a, axis=1),
            jnp.concatenate(b, axis=1),
            NT_DIMS,
            preferred_element_type=jnp.float32,
        )

    zeros = jnp.zeros((field.shape[0], PAD, lanes), jnp.float32)
    field[:, 0:PAD, :] = zeros
    field[:, PAD + size_y :, :] = zeros
    inside = slice(PAD, PAD + size_y)
    top = REACH + size_x

    for copy in copies[1:]:
        copy.wait()
    out = inject(own_a, own_b)
    first = (out[:, 0:lanes] + out[:, lanes : 2 * lanes]).reshape(size_x, size_y, lanes)
    source1[...] = (out[:, 2 * lanes : 3 * lanes] + out[:, 3 * lanes :]).reshape(
        size_x, size_y, lanes
    )
    fresh = free[REACH:top] + scale[REACH:top] * first
    field[REACH:top, inside, :] = fresh
    done = [
        pltpu.make_async_copy(field.at[REACH:top, inside, :], prior_far, out_sems.at[0])
    ]
    done[0].start()
    out = inject(low_a, low_b)
    first = (out[:, 0:lanes] + out[:, lanes:]).reshape(REACH, size_y, lanes)
    field[0:REACH, inside, :] = free[0:REACH] + scale[0:REACH] * first
    out = inject(high_a, high_b)
    first = (out[:, 0:lanes] + out[:, lanes:]).reshape(REACH, size_y, lanes)
    field[top:, inside, :] = free[top:] + scale[top:] * first

    half = size_x // 2
    for part in range(2):
        planes = slice(part * half, (part + 1) * half)

        @pl.loop(part * half, (part + 1) * half)
        def _(x):
            at = x + REACH
            fresh = field[at, inside, :]
            following = (
                2.0 * fresh
                - now[x]
                + scale[at] * (laplacian_plane(field, at, size_y) + source1[x])
            )
            last[x] = following
            gradient[x] = weight0[x] * fresh + weight1[x] * following

        done += started(
            out_sems.at[pl.ds(1 + 2 * part, 2)],
            (last.at[planes], last_far.at[planes]),
            (gradient.at[planes], gradient_far.at[planes]),
        )
    for copy in done:
        copy.wait()


def body(
    synthetic,
    observed,
    offsets,
    lines,
    owners,
    cells,
    taps,
    line_taps,
    velocity,
    adjoint_old,
    adjoint_now,
    forward,
):
    count = synthetic.shape[0]
    size_x, size_y, lanes = velocity.shape
    devices = lax.axis_size("sub")
    cap = max(2, 2 * count // devices)
    f32 = jnp.float32

    pair = [(i, i ^ 1) for i in range(devices)]
    following = [(i, i + 1) for i in range(1, devices - 1, 2)]
    following = following + [(b, a) for a, b in following]

    plane = (size_y, lanes)
    outer = size_x + 2 * REACH
    inner = pltpu.VMEM((size_x,) + plane, f32)
    padded = pltpu.VMEM((outer, size_y + 2 * PAD, lanes), f32)
    halo = pltpu.VMEM((3 * REACH,) + plane, f32)
    wider = pltpu.VMEM((outer,) + plane, f32)
    inner_far = pltpu.HBM((size_x,) + plane, f32)
    wider_far = pltpu.HBM((outer,) + plane, f32)
    dma = pltpu.SemaphoreType.DMA

    row = (1, count)
    traces = (
        synthetic,
        observed,
        offsets.reshape(row),
        lines,
        owners.reshape(row),
        cells.reshape(row),
        taps.reshape(1, -1),
    )
    to_pair, to_next, *traces = pl.pallas_call(
        functools.partial(own_kernel, len(traces)),
        out_shape=(halo, halo) + tuple(pltpu.VMEM(t.shape, t.dtype) for t in traces),
        in_specs=[FAR] * (3 + len(traces)),
        out_specs=(VMEM,) * (2 + len(traces)),
        scratch_shapes=[inner, inner, inner, padded, inner, dma((3 + len(traces),))],
        compiler_params=PARAMS,
        name="own",
    )(*far(adjoint_old, adjoint_now, velocity, *traces))
    from_next = lax.ppermute(to_next, "sub", following)
    from_pair = lax.ppermute(to_pair, "sub", pair)

    send = pl.pallas_call(
        functools.partial(pack_kernel, devices, cap, velocity.size),
        out_shape=jax.ShapeDtypeStruct((devices, 8, LANES), f32),
        in_specs=[FAR] + [VMEM] * len(traces),
        out_specs=VMEM,
        scratch_shapes=[pltpu.SMEM(line_taps.shape, f32), dma((1,))],
        compiler_params=PARAMS,
        name="pack",
    )(*far(line_taps), *(near(t) for t in traces))
    got = lax.all_to_all(send, "sub", split_axis=0, concat_axis=0, tiled=True)

    partial, weight0, weight1 = pl.pallas_call(
        inner_kernel,
        out_shape=(inner_far,) * 3,
        in_specs=[FAR] * 4,
        out_specs=(VMEM,) * 3,
        scratch_shapes=[padded, inner, inner, pltpu.VMEM(forward.shape, f32), dma((4,))],
        compiler_params=PARAMS,
        name="inner",
    )(*far(adjoint_old, adjoint_now, velocity, forward))
    free, scale = pl.pallas_call(
        first_kernel,
        out_shape=(wider_far,) * 2,
        in_specs=[VMEM] * 5,
        out_specs=(VMEM,) * 2,
        compiler_params=PARAMS,
        name="first",
    )(near(from_pair), near(from_next), *far(partial, adjoint_now, velocity))

    field = jax.ShapeDtypeStruct((size_x,) + plane, f32)
    return pl.pallas_call(
        functools.partial(second_kernel, devices, cap),
        out_shape=(field, field, field),
        in_specs=[VMEM] + [FAR] * 6,
        out_specs=(FAR,) * 3,
        scratch_shapes=[
            pltpu.SMEM(line_taps.shape, f32),
            wider,
            wider,
            inner,
            inner,
            inner,
            inner,
            inner,
            pltpu.VMEM((outer, size_y + 2 * PAD, lanes), f32),
            inner,
            dma((6,)),
            dma((5,)),
        ],
        compiler_params=PARAMS,
        name="second",
    )(near(got), *far(line_taps, free, scale, adjoint_now, weight0, weight1))


def solution(mesh):
    return jax.shard_map(
        body,
        mesh=mesh,
        in_specs=(
            P(("shot", "sub"), None),
            P(("shot", "sub"), None),
            P(("shot", "sub")),
            P(None, ("shot", "sub")),
            P(("shot", "sub"), None),
            P(("shot", "sub")),
            P(),
            P(),
            P("sub", None, None),
            P(("shot", "sub"), None, None),
            P(("shot", "sub"), None, None),
            P(None, ("shot", "sub"), None, None),
        ),
        out_specs=(
            P(("shot", "sub"), None, None),
            P(("shot", "sub"), None, None),
            P(("shot", "sub"), None, None),
        ),
        check_vma=False,
    )
```

```python
import functools

import jax
import jax.numpy as jnp
from jax import lax
from jax.experimental import pallas as pl
from jax.experimental.pallas import tpu as pltpu
from jax.sharding import PartitionSpec as P

SW = 4
STEPS = 2
REACH = 4
LANES = 128
EDGE = 2 * SW

COEF = (-205.0 / 72.0, 8.0 / 5.0, -1.0 / 5.0, 8.0 / 315.0, -1.0 / 560.0)
DT_OVER_H = 0.18

VMEM = pl.BlockSpec(memory_space=pltpu.VMEM)
FAR = pl.BlockSpec(memory_space=pltpu.HBM)
PARAMS = pltpu.CompilerParams(vmem_limit_bytes=16 * 2**20)
NT_DIMS = (((1,), (1,)), ((), ()))


def near(array):
    return pltpu.with_memory_space_constraint(array, pltpu.VMEM)


def far(*arrays):
    return [pltpu.with_memory_space_constraint(array, pltpu.HBM) for array in arrays]


def started(sems, *pairs):
    copies = [
        pltpu.make_async_copy(source, target, sems.at[i])
        for i, (source, target) in enumerate(pairs)
    ]
    for copy in copies:
        copy.start()
    return copies


def parts_of(value, count):
    parts = []
    for _ in range(count):
        part = value.astype(jnp.bfloat16).astype(jnp.float32)
        parts.append(part)
        value = value - part
    return parts


def iota(shape, axis):
    return lax.broadcasted_iota(jnp.int32, shape, axis)


PACKED = 16


def across16(row):
    return jnp.broadcast_to(row, (PACKED, row.shape[1])).astype(jnp.int16)[None]


def index16(count, width):
    rows = iota((count, width), 0).astype(jnp.int16)
    return rows.reshape(count // PACKED, PACKED, width)


def same16(index, row):
    return index == across16(row)


def pick16(mask, row):
    width = row.shape[1]
    wide = jnp.broadcast_to(row, (PACKED, width)).astype(jnp.bfloat16)
    picked = jnp.where(mask, wide[None], jnp.zeros((), jnp.bfloat16))
    return picked.reshape(-1, width)


def hot16(index, row):
    return pick16(same16(index, row), jnp.ones(row.shape, jnp.float32))


PAD = 8


def laplacian_plane(field, x, size_y):
    centre = field[x, PAD : PAD + size_y, :]
    lanes = centre.shape[1]
    lane = iota(centre.shape, 1)
    total = 3.0 * COEF[0] * centre
    for k in range(1, 5):
        near = field[x + k, PAD : PAD + size_y, :] + field[x - k, PAD : PAD + size_y, :]
        near = near + field[x, PAD + k : PAD + k + size_y, :]
        near = near + field[x, PAD - k : PAD - k + size_y, :]
        near = near + jnp.where(lane < lanes - k, pltpu.roll(centre, lanes - k, 1), 0.0)
        near = near + jnp.where(lane >= k, pltpu.roll(centre, k, 1), 0.0)
        total = total + COEF[k] * near
    return total


def squared(speed):
    factor = DT_OVER_H * speed
    return factor * factor


def send_kernel(
    devices,
    cap,
    block,
    own_far,
    cells_far,
    taps_far,
    off_far,
    lines_far,
    line_taps_far,
    syn_far,
    obs_far,
    now_far,
    vel_far,
    old_far,
    send_far,
    to_pair,
    to_next,
    own,
    cells,
    taps,
    off,
    lines,
    line_taps,
    syn,
    obs,
    old,
    vel,
    wide,
    send,
    sems,
):
    size_x, size_y, lanes = old.shape
    inside = slice(PAD, PAD + size_y)
    copies = started(
        sems,
        (own_far, own),
        (cells_far, cells),
        (taps_far, taps),
        (off_far, off),
        (lines_far, lines),
        (line_taps_far, line_taps),
        (syn_far, syn),
        (obs_far, obs),
        (now_far, wide.at[REACH : REACH + size_x, inside, :]),
        (vel_far, vel),
        (old_far, old),
    )
    edge = jnp.zeros((wide.shape[0], PAD, lanes), jnp.float32)
    wide[:, 0:PAD, :] = edge
    wide[:, PAD + size_y :, :] = edge
    blank = jnp.zeros((REACH, size_y, lanes), jnp.float32)
    wide[0:REACH, inside, :] = blank
    wide[REACH + size_x :, inside, :] = blank
    for copy in copies[:6]:
        copy.wait()
    me = lax.axis_index("sub")
    count, samples = syn.shape
    ntap = taps.shape[1]
    pack = LANES // cap
    group = LANES // EDGE
    place = iota((1, count), 1)
    owner = own[...]
    owned = same16(index16(devices, count), owner)
    one_hot = pick16(owned, jnp.ones((1, count), jnp.float32))
    chunks = [one_hot[:, at : at + LANES] for at in range(0, count, LANES)]
    ahead = index16(LANES, LANES) < across16(iota((1, LANES), 1))
    ranks = jnp.dot(
        jnp.concatenate(chunks, axis=0),
        pick16(ahead, jnp.ones((1, LANES), jnp.float32)),
        preferred_element_type=jnp.float32,
    )
    base = jnp.zeros((devices, 1), jnp.float32)
    rank = []
    for i, chunk in enumerate(chunks):
        chunk = chunk.astype(jnp.float32)
        rank.append(
            jnp.sum(
                chunk * (ranks[i * devices : (i + 1) * devices] + base), axis=0, keepdims=True
            )
        )
        base = base + jnp.sum(chunk, axis=1, keepdims=True)
    rank = jnp.concatenate(rank, axis=1).astype(jnp.int32)
    lane = index16(LANES, count)
    slot = hot16(lane, rank + (me % pack) * cap)
    edge_lane = jnp.where(
        place < SW, place, jnp.where(place >= count - SW, place - count + EDGE, -LANES)
    )
    chosen = hot16(lane, edge_lane + (me % group) * EDGE)

    row = jnp.concatenate([taps[...], jnp.zeros((1, samples - ntap), jnp.float32)], axis=1)
    starts = -(-(samples - ntap + 1) // 8) * 8
    toeplitz = pltpu.roll(
        jnp.broadcast_to(row, (starts, samples)), 0, 1, stride=1, stride_axis=0
    )
    for copy in copies[6:8]:
        copy.wait()
    all_starts = lax.dot_general(
        toeplitz,
        syn[...] - obs[...],
        NT_DIMS,
        precision=lax.Precision.HIGHEST,
        preferred_element_type=jnp.float32,
    )
    start = iota((starts, count), 0)
    offset = off[...]
    filtered = [
        jnp.sum(jnp.where(start == offset + step, all_starts, 0.0), axis=0, keepdims=True)
        for step in range(STEPS)
    ]
    both = jnp.concatenate(filtered + [jnp.zeros((8 - STEPS, count), jnp.float32)], axis=0)
    before = lines[0:1, :]
    after = lines[1:2, :]
    sources = jnp.zeros((8, count), jnp.float32)
    for reach in range(-SW, SW + 1):
        term = line_taps[0:1, reach + SW : reach + SW + 1] * (
            pltpu.roll(both, (-reach) % count, 1) if reach else both
        )
        if reach < 0:
            keep = (before >= -reach) & (place >= -reach)
        elif reach > 0:
            keep = (after >= reach) & (place < count - reach)
        else:
            keep = before >= 0
        sources = sources + jnp.where(keep, term, 0.0)
    cell = cells[...]
    high = (cell >> 8).astype(jnp.float32)
    low = (cell & 255).astype(jnp.float32)
    pieces = parts_of(sources[0:1], 3) + parts_of(sources[1:2], 3) + [high, low]
    spread = jnp.concatenate([pick16(owned, piece) for piece in pieces], axis=0)
    out = lax.dot_general(spread, slot, NT_DIMS, preferred_element_type=jnp.float32)
    part = [out[k * devices : (k + 1) * devices] for k in range(8)]
    value0 = part[0] + part[1] + part[2]
    value1 = part[3] + part[4] + part[5]
    where = 256.0 * part[6] + part[7]
    none = jnp.zeros((1, LANES), jnp.float32)

    def to_upper(rows):
        return pltpu.roll(jnp.concatenate([none, rows[:-1]], axis=0), LANES // 2, 1)

    def to_lower(rows):
        return pltpu.roll(jnp.concatenate([rows[1:], none], axis=0), LANES // 2, 1)

    send[:, 0, :] = value0 + to_upper(value0)
    send[:, 1, :] = where + to_upper(where)
    send[:, 2, :] = value1 + to_lower(value0)
    send[:, 3, :] = to_lower(where)
    count_ = jnp.where(place < SW, before, after).astype(jnp.float32)
    edge_rows = (
        parts_of(both[0:1], 3)
        + parts_of(both[1:2], 3)
        + [owner.astype(jnp.float32), high, low, count_]
    )
    edge_rows = jnp.concatenate(
        edge_rows + [jnp.zeros((16 - len(edge_rows), count), jnp.float32)], axis=0
    ).astype(jnp.bfloat16)
    edge = lax.dot_general(edge_rows, chosen, NT_DIMS, preferred_element_type=jnp.float32)
    edge_cell = edge[6:7] * float(block) + 256.0 * edge[7:8] + edge[8:9]
    shape = (devices, LANES)
    send[:, 4, :] = jnp.broadcast_to(edge[0:1] + edge[1:2] + edge[2:3], shape)
    send[:, 5, :] = jnp.broadcast_to(edge[3:4] + edge[4:5] + edge[5:6], shape)
    send[:, 6, :] = jnp.broadcast_to(edge_cell, shape)
    send[:, 7, :] = jnp.broadcast_to(edge[9:10], shape)
    sent = pltpu.make_async_copy(send, send_far, sems.at[11])
    sent.start()
    for copy in copies[8:]:
        copy.wait()
    odd = me % 2

    def half(target, start):
        for i in range(REACH):
            x = start + i
            own_now = wide[REACH + x, inside, :]
            speed = vel[x]
            target[i] = own_now
            target[REACH + i] = (
                2.0 * own_now
                - old[x]
                + squared(speed) * laplacian_plane(wide, x + REACH, size_y)
            )
            target[2 * REACH + i] = speed

    far_half = size_x - REACH
    half(to_next, far_half * odd)
    half(to_pair, far_half * (1 - odd))
    sent.wait()


def inner_kernel(old_far, now_far, vel_far, fwd_far, partial, now, vel, weight0, weight1, wide, old, fwd, sems):
    size_x, size_y, lanes = old.shape
    inside = slice(PAD, PAD + size_y)
    copies = started(
        sems,
        (now_far, wide.at[REACH : REACH + size_x, inside, :]),
        (vel_far, vel),
        (old_far, old),
        (fwd_far, fwd),
    )
    edge = jnp.zeros((wide.shape[0], PAD, lanes), jnp.float32)
    wide[:, 0:PAD, :] = edge
    wide[:, PAD + size_y :, :] = edge
    blank = jnp.zeros((REACH, size_y, lanes), jnp.float32)
    wide[0:REACH, inside, :] = blank
    wide[REACH + size_x :, inside, :] = blank
    for copy in copies:
        copy.wait()

    for x in range(size_x):
        speed = vel[x]
        now[x] = wide[REACH + x, inside, :]
        partial[x] = (
            2.0 * now[x]
            - old[x]
            + squared(speed) * laplacian_plane(wide, x + REACH, size_y)
        )
        weight = 2.0 / (speed * speed * speed)
        f1 = fwd[1, x]
        f2 = fwd[2, x]
        weight0[x] = weight * (fwd[0, x] - 2.0 * f1 + f2)
        weight1[x] = weight * (f1 - 2.0 * f2 + fwd[3, x])


def across(field, x, low, high):
    total = None
    for k in range(1, 5):
        for at in (x - k, x + k):
            if low <= at < high:
                term = COEF[k] * field[at - low]
                total = term if total is None else total + term
    return total


def first_kernel(
    from_pair, from_next, partial, now, vel, free, scale
):
    odd = lax.axis_index("sub") % 2
    size_x = now.shape[0]
    top = REACH + size_x

    def border(source, first_out, low):
        for i in range(REACH):
            factor = squared(source[2 * REACH + i])
            scale[first_out + i] = factor
            free[first_out + i] = source[REACH + i] + factor * across(now, low + i, 0, size_x)
        planes = range(REACH) if low < 0 else range(size_x - REACH, size_x)
        for x in planes:
            factor = squared(vel[x])
            scale[REACH + x] = factor
            free[REACH + x] = partial[x] + factor * across(source, x, low, low + REACH)

    @pl.when(odd == 0)
    def _():
        border(from_next, 0, -REACH)
        border(from_pair, top, size_x)

    @pl.when(odd == 1)
    def _():
        border(from_pair, 0, -REACH)
        border(from_next, top, size_x)


def second_kernel(
    devices,
    cap,
    got,
    free,
    scale,
    line_taps_far,
    now_far,
    weight0_far,
    weight1_far,
    prior_far,
    last_far,
    gradient_far,
    line_taps,
    now,
    weight0,
    weight1,
    last,
    gradient,
    field,
    source1,
    sems,
    out_sems,
):
    copies = started(
        sems,
        (line_taps_far, line_taps),
        (now_far, now),
        (weight0_far, weight0),
        (weight1_far, weight1),
    )
    me = lax.axis_index("sub")
    size_x, size_y, lanes = now.shape
    rows = size_x * size_y
    halo = REACH * size_y
    block = rows * lanes
    pack = LANES // cap
    lane8 = iota((8, LANES), 1)
    shift = lanes.bit_length() - 1

    def hot_rows(cell, move, index):
        return hot16(index, (cell >> shift) + move)

    def spread(cell, values):
        at = same16(zs, cell & (lanes - 1))
        stack = []
        for value in values:
            for part in parts_of(value, 2):
                stack.append(pick16(at, part))
        return jnp.concatenate(stack, axis=0)

    def inject(a, b):
        return lax.dot_general(
            jnp.concatenate(a, axis=1),
            jnp.concatenate(b, axis=1),
            NT_DIMS,
            preferred_element_type=jnp.float32,
        )

    zs = index16(LANES, LANES)
    row_index = index16(rows, LANES)
    halo_index = index16(halo, LANES)

    own_a, own_b, low_a, low_b, high_a, high_b = [], [], [], [], [], []
    mine, other = [], []
    for g in range(devices // pack):
        tiles = [got[g * pack + q] for q in range(pack)]
        one, two = tiles[0], tiles[pack // 2]
        for q in range(1, pack):
            later = lane8 >= q * cap
            one = jnp.where(later, tiles[q], one)
            two = jnp.where(later, tiles[(q + pack // 2) % pack], two)
        mine.append(one)
        other.append(two)
    for one in mine:
        cell = one[1:2].astype(jnp.int32)
        own_a.append(hot_rows(cell, 0, row_index))
        own_b.append(spread(cell, [one[0:1], one[2:3]]))
    for two in other:
        cell = two[1:2].astype(jnp.int32)
        low_a.append(hot_rows(cell, halo - rows, halo_index))
        low_b.append(spread(cell, [two[0:1]]))
    for two in other:
        cell = two[3:4].astype(jnp.int32)
        high_a.append(hot_rows(cell, 0, halo_index))
        high_b.append(spread(cell, [two[2:3]]))

    group = LANES // EDGE
    edge_parts = []
    for g in range(-(-devices // group)):
        total = got[g * group]
        for i in range(g * group + 1, min(devices, (g + 1) * group)):
            total = total + got[i]
        edge_parts.append(total)
    edge = jnp.concatenate(edge_parts, axis=1)
    width = edge.shape[1]
    spot = iota((8, width), 1)
    e = spot % EDGE
    count = edge[7:8]
    missing = jnp.zeros((8, width), jnp.float32)
    copies[0].wait()
    for reach in range(-SW, SW + 1):
        if reach == 0:
            continue
        if reach < 0:
            crosses = (e < -reach) & (spot >= -reach)
        else:
            crosses = (e >= EDGE - reach) & (spot < width - reach)
        keep = crosses & (count >= float(abs(reach)))
        missing = missing + jnp.where(
            keep, line_taps[reach + SW] * pltpu.roll(edge, (-reach) % width, 1), 0.0
        )
    edge_cell = edge[6:7].astype(jnp.int32) - me * block
    edge_row = jnp.clip(edge_cell >> shift, -2 * rows, 2 * rows)
    for g in range(width // LANES):
        at = slice(g * LANES, (g + 1) * LANES)
        b = spread(edge_cell[:, at], [missing[4:5, at], missing[5:6, at]])
        own_a.append(hot16(row_index, edge_row[:, at]))
        own_b.append(b)
        low_a.append(hot16(halo_index, edge_row[:, at] + halo))
        low_b.append(b[: 2 * LANES])
        high_a.append(hot16(halo_index, edge_row[:, at] - rows))
        high_b.append(b[: 2 * LANES])

    zeros = jnp.zeros((field.shape[0], PAD, lanes), jnp.float32)
    field[:, 0:PAD, :] = zeros
    field[:, PAD + size_y :, :] = zeros
    inside = slice(PAD, PAD + size_y)
    top = REACH + size_x

    out = inject(own_a, own_b)
    low_out = inject(low_a, low_b)
    high_out = inject(high_a, high_b)
    for copy in copies[1:]:
        copy.wait()
    first = (out[:, 0:lanes] + out[:, lanes : 2 * lanes]).reshape(size_x, size_y, lanes)
    source1[...] = (out[:, 2 * lanes : 3 * lanes] + out[:, 3 * lanes :]).reshape(
        size_x, size_y, lanes
    )
    field[REACH:top, inside, :] = free[REACH:top] + scale[REACH:top] * first
    done = [
        pltpu.make_async_copy(field.at[REACH:top, inside, :], prior_far, out_sems.at[0])
    ]
    done[0].start()
    first = (low_out[:, 0:lanes] + low_out[:, lanes:]).reshape(REACH, size_y, lanes)
    field[0:REACH, inside, :] = free[0:REACH] + scale[0:REACH] * first
    first = (high_out[:, 0:lanes] + high_out[:, lanes:]).reshape(REACH, size_y, lanes)
    field[top:, inside, :] = free[top:] + scale[top:] * first

    half = size_x // 2
    for part in range(2):
        planes = slice(part * half, (part + 1) * half)

        for x in range(part * half, (part + 1) * half):
            at = x + REACH
            fresh = field[at, inside, :]
            following = (
                2.0 * fresh
                - now[x]
                + scale[at] * (laplacian_plane(field, at, size_y) + source1[x])
            )
            last[x] = following
            gradient[x] = weight0[x] * fresh + weight1[x] * following

        done += started(
            out_sems.at[pl.ds(1 + 2 * part, 2)],
            (last.at[planes], last_far.at[planes]),
            (gradient.at[planes], gradient_far.at[planes]),
        )
    for copy in done:
        copy.wait()


def body(
    synthetic,
    observed,
    offsets,
    lines,
    owners,
    cells,
    taps,
    line_taps,
    velocity,
    adjoint_old,
    adjoint_now,
    forward,
):
    count = synthetic.shape[0]
    size_x, size_y, lanes = velocity.shape
    devices = lax.axis_size("sub")
    cap = max(2, 2 * count // devices)
    f32 = jnp.float32

    pair = [(i, i ^ 1) for i in range(devices)]
    following = [(i, i + 1) for i in range(1, devices - 1, 2)]
    following = following + [(b, a) for a, b in following]

    plane = (size_y, lanes)
    outer = size_x + 2 * REACH
    inner = pltpu.VMEM((size_x,) + plane, f32)
    padded = pltpu.VMEM((outer, size_y + 2 * PAD, lanes), f32)
    halo = pltpu.VMEM((3 * REACH,) + plane, f32)
    wider = pltpu.VMEM((outer,) + plane, f32)
    inner_far = pltpu.HBM((size_x,) + plane, f32)
    wider_far = pltpu.HBM((outer,) + plane, f32)
    dma = pltpu.SemaphoreType.DMA

    row = (1, count)
    small = pltpu.VMEM(row, jnp.int32)
    traces = pltpu.VMEM(synthetic.shape, f32)
    send, to_pair, to_next = pl.pallas_call(
        functools.partial(send_kernel, devices, cap, velocity.size),
        out_shape=(pltpu.HBM((devices, 8, LANES), f32), halo, halo),
        in_specs=[FAR] * 11,
        out_specs=(FAR, VMEM, VMEM),
        scratch_shapes=[
            small,
            small,
            pltpu.VMEM((1, taps.shape[0]), f32),
            small,
            pltpu.VMEM(lines.shape, jnp.int32),
            pltpu.VMEM((1, line_taps.shape[0]), f32),
            traces,
            traces,
            inner,
            inner,
            padded,
            pltpu.VMEM((devices, 8, LANES), f32),
            dma((12,)),
        ],
        compiler_params=PARAMS,
        name="send",
    )(
        *far(
            owners.reshape(row),
            cells.reshape(row),
            taps.reshape(1, -1),
            offsets.reshape(row),
            lines,
            line_taps.reshape(1, -1),
            synthetic,
            observed,
            adjoint_now,
            velocity,
            adjoint_old,
        )
    )
    from_next = lax.ppermute(to_next, "sub", following)
    from_pair = lax.ppermute(to_pair, "sub", pair)
    got = lax.all_to_all(send, "sub", split_axis=0, concat_axis=0, tiled=True)

    partial, now, vel, weight0, weight1 = pl.pallas_call(
        inner_kernel,
        out_shape=(inner,) * 3 + (inner_far,) * 2,
        in_specs=[FAR] * 4,
        out_specs=(VMEM,) * 5,
        scratch_shapes=[padded, inner, pltpu.VMEM(forward.shape, f32), dma((4,))],
        compiler_params=PARAMS,
        name="inner",
    )(*far(adjoint_old, adjoint_now, velocity, forward))
    free, scale = pl.pallas_call(
        first_kernel,
        out_shape=(wider,) * 2,
        in_specs=[VMEM] * 5,
        out_specs=(VMEM,) * 2,
        compiler_params=PARAMS,
        name="first",
    )(near(from_pair), near(from_next), near(partial), near(now), near(vel))

    field = jax.ShapeDtypeStruct((size_x,) + plane, f32)
    return pl.pallas_call(
        functools.partial(second_kernel, devices, cap),
        out_shape=(field, field, field),
        in_specs=[VMEM] * 3 + [FAR] * 4,
        out_specs=(FAR,) * 3,
        scratch_shapes=[
            pltpu.SMEM(line_taps.shape, f32),
            inner,
            inner,
            inner,
            inner,
            inner,
            pltpu.VMEM((outer, size_y + 2 * PAD, lanes), f32),
            inner,
            dma((4,)),
            dma((5,)),
        ],
        compiler_params=PARAMS,
        name="second",
    )(
        near(got),
        near(free),
        near(scale),
        *far(line_taps, adjoint_now, weight0, weight1),
    )


def solution(mesh):
    return jax.shard_map(
        body,
        mesh=mesh,
        in_specs=(
            P(("shot", "sub"), None),
            P(("shot", "sub"), None),
            P(("shot", "sub")),
            P(None, ("shot", "sub")),
            P(("shot", "sub"), None),
            P(("shot", "sub")),
            P(),
            P(),
            P("sub", None, None),
            P(("shot", "sub"), None, None),
            P(("shot", "sub"), None, None),
            P(None, ("shot", "sub"), None, None),
        ),
        out_specs=(
            P(("shot", "sub"), None, None),
            P(("shot", "sub"), None, None),
            P(("shot", "sub"), None, None),
        ),
        check_vma=False,
    )
```

```python
import functools

import jax
import jax.numpy as jnp
from jax import lax
from jax.experimental import pallas as pl
from jax.experimental.pallas import tpu as pltpu
from jax.sharding import PartitionSpec as P

SW = 4
STEPS = 2
REACH = 4
LANES = 128
EDGE = 2 * SW

COEF = (-205.0 / 72.0, 8.0 / 5.0, -1.0 / 5.0, 8.0 / 315.0, -1.0 / 560.0)
DT_OVER_H = 0.18

VMEM = pl.BlockSpec(memory_space=pltpu.VMEM)
FAR = pl.BlockSpec(memory_space=pltpu.HBM)
PARAMS = pltpu.CompilerParams(vmem_limit_bytes=16 * 2**20)
NT_DIMS = (((1,), (1,)), ((), ()))


def near(array):
    return pltpu.with_memory_space_constraint(array, pltpu.VMEM)


def far(*arrays):
    return [pltpu.with_memory_space_constraint(array, pltpu.HBM) for array in arrays]


def started(sems, *pairs):
    copies = [
        pltpu.make_async_copy(source, target, sems.at[i])
        for i, (source, target) in enumerate(pairs)
    ]
    for copy in copies:
        copy.start()
    return copies


def parts_of(value, count):
    parts = []
    for _ in range(count):
        part = value.astype(jnp.bfloat16).astype(jnp.float32)
        parts.append(part)
        value = value - part
    return parts


def iota(shape, axis):
    return lax.broadcasted_iota(jnp.int32, shape, axis)


PACKED = 16


def across16(row):
    return jnp.broadcast_to(row, (PACKED, row.shape[1])).astype(jnp.int16)[None]


def index16(count, width):
    rows = iota((count, width), 0).astype(jnp.int16)
    return rows.reshape(count // PACKED, PACKED, width)


def same16(index, row):
    return index == across16(row)


def pick16(mask, row):
    width = row.shape[1]
    wide = jnp.broadcast_to(row, (PACKED, width)).astype(jnp.bfloat16)
    picked = jnp.where(mask, wide[None], jnp.zeros((), jnp.bfloat16))
    return picked.reshape(-1, width)


def hot16(index, row):
    return pick16(same16(index, row), jnp.ones(row.shape, jnp.float32))


PAD = 8


def laplacian_plane(field, x, size_y):
    centre = field[x, PAD : PAD + size_y, :]
    lanes = centre.shape[1]
    lane = iota(centre.shape, 1)
    total = 3.0 * COEF[0] * centre
    for k in range(1, 5):
        near = field[x + k, PAD : PAD + size_y, :] + field[x - k, PAD : PAD + size_y, :]
        near = near + field[x, PAD + k : PAD + k + size_y, :]
        near = near + field[x, PAD - k : PAD - k + size_y, :]
        near = near + jnp.where(lane < lanes - k, pltpu.roll(centre, lanes - k, 1), 0.0)
        near = near + jnp.where(lane >= k, pltpu.roll(centre, k, 1), 0.0)
        total = total + COEF[k] * near
    return total


def squared(speed):
    factor = DT_OVER_H * speed
    return factor * factor


def send_kernel(
    devices,
    cap,
    block,
    own_far,
    cells_far,
    taps_far,
    off_far,
    lines_far,
    line_taps_far,
    syn_far,
    obs_far,
    now_far,
    vel_far,
    old_far,
    send_far,
    to_pair,
    to_next,
    own,
    cells,
    taps,
    off,
    lines,
    line_taps,
    syn,
    obs,
    old,
    vel,
    wide,
    send,
    sems,
):
    size_x, size_y, lanes = old.shape
    inside = slice(PAD, PAD + size_y)
    copies = started(
        sems,
        (own_far, own),
        (taps_far, taps),
        (syn_far, syn),
        (obs_far, obs),
        (cells_far, cells),
        (off_far, off),
        (lines_far, lines),
        (line_taps_far, line_taps),
        (now_far, wide.at[REACH : REACH + size_x, inside, :]),
        (vel_far, vel),
        (old_far, old),
    )
    edge = jnp.zeros((wide.shape[0], PAD, lanes), jnp.float32)
    wide[:, 0:PAD, :] = edge
    wide[:, PAD + size_y :, :] = edge
    blank = jnp.zeros((REACH, size_y, lanes), jnp.float32)
    wide[0:REACH, inside, :] = blank
    wide[REACH + size_x :, inside, :] = blank
    for copy in copies[:2]:
        copy.wait()
    me = lax.axis_index("sub")
    count, samples = syn.shape
    ntap = taps.shape[1]
    pack = LANES // cap
    group = LANES // EDGE
    place = iota((1, count), 1)
    owner = own[...]
    owned = same16(index16(devices, count), owner)
    one_hot = pick16(owned, jnp.ones((1, count), jnp.float32))
    chunks = [one_hot[:, at : at + LANES] for at in range(0, count, LANES)]
    ahead = index16(LANES, LANES) < across16(iota((1, LANES), 1))
    ranks = jnp.dot(
        jnp.concatenate(chunks, axis=0),
        pick16(ahead, jnp.ones((1, LANES), jnp.float32)),
        preferred_element_type=jnp.float32,
    )
    base = jnp.zeros((devices, 1), jnp.float32)
    rank = []
    for i, chunk in enumerate(chunks):
        chunk = chunk.astype(jnp.float32)
        rank.append(
            jnp.sum(
                chunk * (ranks[i * devices : (i + 1) * devices] + base), axis=0, keepdims=True
            )
        )
        base = base + jnp.sum(chunk, axis=1, keepdims=True)
    rank = jnp.concatenate(rank, axis=1).astype(jnp.int32)
    lane = index16(LANES, count)
    slot = hot16(lane, rank + (me % pack) * cap)
    edge_lane = jnp.where(
        place < SW, place, jnp.where(place >= count - SW, place - count + EDGE, -LANES)
    )
    chosen = hot16(lane, edge_lane + (me % group) * EDGE)

    row = jnp.concatenate([taps[...], jnp.zeros((1, samples - ntap), jnp.float32)], axis=1)
    starts = -(-(samples - ntap + 1) // 16) * 16
    toeplitz = pltpu.roll(
        jnp.broadcast_to(row, (starts, samples)), 0, 1, stride=1, stride_axis=0
    )
    for copy in copies[2:-3]:
        copy.wait()
    residual = syn[...] - obs[...]
    r_high = residual.astype(jnp.bfloat16)
    r_low = (residual - r_high.astype(jnp.float32)).astype(jnp.bfloat16)
    t_high = toeplitz.astype(jnp.bfloat16)
    t_low = (toeplitz - t_high.astype(jnp.float32)).astype(jnp.bfloat16)
    all_starts = sum(
        lax.dot_general(a, b, NT_DIMS, preferred_element_type=jnp.float32)
        for a, b in ((t_high, r_low), (t_low, r_high), (t_high, r_high))
    )
    start = iota((starts, count), 0)
    offset = off[...]
    filtered = [
        jnp.sum(jnp.where(start == offset + step, all_starts, 0.0), axis=0, keepdims=True)
        for step in range(STEPS)
    ]
    both = jnp.concatenate(filtered + [jnp.zeros((8 - STEPS, count), jnp.float32)], axis=0)
    before = lines[0:1, :]
    after = lines[1:2, :]
    sources = jnp.zeros((8, count), jnp.float32)
    for reach in range(-SW, SW + 1):
        term = line_taps[0:1, reach + SW : reach + SW + 1] * (
            pltpu.roll(both, (-reach) % count, 1) if reach else both
        )
        if reach < 0:
            keep = (before >= -reach) & (place >= -reach)
        elif reach > 0:
            keep = (after >= reach) & (place < count - reach)
        else:
            keep = before >= 0
        sources = sources + jnp.where(keep, term, 0.0)
    cell = cells[...]
    high = (cell >> 8).astype(jnp.float32)
    low = (cell & 255).astype(jnp.float32)
    pieces = parts_of(sources[0:1], 3) + parts_of(sources[1:2], 3) + [high, low]
    spread = jnp.concatenate([pick16(owned, piece) for piece in pieces], axis=0)
    out = lax.dot_general(spread, slot, NT_DIMS, preferred_element_type=jnp.float32)
    part = [out[k * devices : (k + 1) * devices] for k in range(8)]
    value0 = part[0] + part[1] + part[2]
    value1 = part[3] + part[4] + part[5]
    where = 256.0 * part[6] + part[7]
    none = jnp.zeros((1, LANES), jnp.float32)

    def to_upper(rows):
        return pltpu.roll(jnp.concatenate([none, rows[:-1]], axis=0), LANES // 2, 1)

    def to_lower(rows):
        return pltpu.roll(jnp.concatenate([rows[1:], none], axis=0), LANES // 2, 1)

    send[:, 0, :] = value0 + to_upper(value0)
    send[:, 1, :] = where + to_upper(where)
    send[:, 2, :] = value1 + to_lower(value0)
    send[:, 3, :] = to_lower(where)
    count_ = jnp.where(place < SW, before, after).astype(jnp.float32)
    edge_rows = (
        parts_of(both[0:1], 3)
        + parts_of(both[1:2], 3)
        + [owner.astype(jnp.float32), high, low, count_]
    )
    edge_rows = jnp.concatenate(
        edge_rows + [jnp.zeros((16 - len(edge_rows), count), jnp.float32)], axis=0
    ).astype(jnp.bfloat16)
    edge = lax.dot_general(edge_rows, chosen, NT_DIMS, preferred_element_type=jnp.float32)
    edge_cell = edge[6:7] * float(block) + 256.0 * edge[7:8] + edge[8:9]
    shape = (devices, LANES)
    send[:, 4, :] = jnp.broadcast_to(edge[0:1] + edge[1:2] + edge[2:3], shape)
    send[:, 5, :] = jnp.broadcast_to(edge[3:4] + edge[4:5] + edge[5:6], shape)
    send[:, 6, :] = jnp.broadcast_to(edge_cell, shape)
    send[:, 7, :] = jnp.broadcast_to(edge[9:10], shape)
    sent = pltpu.make_async_copy(send, send_far, sems.at[len(copies)])
    sent.start()
    for copy in copies[-3:]:
        copy.wait()
    odd = me % 2

    def half(target, start):
        for i in range(REACH):
            x = start + i
            own_now = wide[REACH + x, inside, :]
            speed = vel[x]
            target[i] = own_now
            target[REACH + i] = (
                2.0 * own_now
                - old[x]
                + squared(speed) * laplacian_plane(wide, x + REACH, size_y)
            )
            target[2 * REACH + i] = speed

    far_half = size_x - REACH
    half(to_next, far_half * odd)
    half(to_pair, far_half * (1 - odd))
    sent.wait()


def inner_kernel(
    old_far,
    now_far,
    vel_far,
    fwd_far,
    line_taps_far,
    partial,
    now,
    vel,
    weight0,
    weight1,
    line_taps,
    wide,
    old,
    fwd,
    sems,
):
    size_x, size_y, lanes = old.shape
    inside = slice(PAD, PAD + size_y)
    copies = started(
        sems,
        (now_far, wide.at[REACH : REACH + size_x, inside, :]),
        (vel_far, vel),
        (old_far, old),
        (fwd_far, fwd),
        (line_taps_far, line_taps),
    )
    edge = jnp.zeros((wide.shape[0], PAD, lanes), jnp.float32)
    wide[:, 0:PAD, :] = edge
    wide[:, PAD + size_y :, :] = edge
    blank = jnp.zeros((REACH, size_y, lanes), jnp.float32)
    wide[0:REACH, inside, :] = blank
    wide[REACH + size_x :, inside, :] = blank
    for copy in copies:
        copy.wait()

    for x in range(size_x):
        speed = vel[x]
        now[x] = wide[REACH + x, inside, :]
        partial[x] = (
            2.0 * now[x]
            - old[x]
            + squared(speed) * laplacian_plane(wide, x + REACH, size_y)
        )
        weight = 2.0 / (speed * speed * speed)
        f1 = fwd[1, x]
        f2 = fwd[2, x]
        weight0[x] = weight * (fwd[0, x] - 2.0 * f1 + f2)
        weight1[x] = weight * (f1 - 2.0 * f2 + fwd[3, x])


def across(field, x, low, high):
    total = None
    for k in range(1, 5):
        for at in (x - k, x + k):
            if low <= at < high:
                term = COEF[k] * field[at - low]
                total = term if total is None else total + term
    return total


def first_kernel(
    from_pair, from_next, partial, now, vel, free, scale
):
    odd = lax.axis_index("sub") % 2
    size_x = now.shape[0]
    top = REACH + size_x

    def border(source, first_out, low):
        for i in range(REACH):
            factor = squared(source[2 * REACH + i])
            scale[first_out + i] = factor
            free[first_out + i] = source[REACH + i] + factor * across(now, low + i, 0, size_x)
        planes = range(REACH) if low < 0 else range(size_x - REACH, size_x)
        for x in planes:
            factor = squared(vel[x])
            scale[REACH + x] = factor
            free[REACH + x] = partial[x] + factor * across(source, x, low, low + REACH)

    @pl.when(odd == 0)
    def _():
        border(from_next, 0, -REACH)
        border(from_pair, top, size_x)

    @pl.when(odd == 1)
    def _():
        border(from_pair, 0, -REACH)
        border(from_next, top, size_x)


def second_kernel(
    devices,
    cap,
    got,
    free,
    scale,
    now,
    weight0,
    weight1,
    line_taps,
    prior_far,
    last_far,
    gradient_far,
    last,
    gradient,
    field,
    source1,
    out_sems,
):
    me = lax.axis_index("sub")
    size_x, size_y, lanes = now.shape
    rows = size_x * size_y
    halo = REACH * size_y
    block = rows * lanes
    pack = LANES // cap
    lane8 = iota((8, LANES), 1)
    shift = lanes.bit_length() - 1

    def hot_rows(cell, move, index):
        return hot16(index, (cell >> shift) + move)

    def spread(cell, values):
        at = same16(zs, cell & (lanes - 1))
        stack = []
        for value in values:
            for part in parts_of(value, 2):
                stack.append(pick16(at, part))
        return jnp.concatenate(stack, axis=0)

    def inject(a, b):
        return lax.dot_general(
            jnp.concatenate(a, axis=1),
            jnp.concatenate(b, axis=1),
            NT_DIMS,
            preferred_element_type=jnp.float32,
        )

    zs = index16(LANES, LANES)
    row_index = index16(rows, LANES)
    halo_index = index16(halo, LANES)

    own_a, own_b, low_a, low_b, high_a, high_b = [], [], [], [], [], []
    mine, other = [], []
    for g in range(devices // pack):
        tiles = [got[g * pack + q] for q in range(pack)]
        one, two = tiles[0], tiles[pack // 2]
        for q in range(1, pack):
            later = lane8 >= q * cap
            one = jnp.where(later, tiles[q], one)
            two = jnp.where(later, tiles[(q + pack // 2) % pack], two)
        mine.append(one)
        other.append(two)
    for one in mine:
        cell = one[1:2].astype(jnp.int32)
        own_a.append(hot_rows(cell, 0, row_index))
        own_b.append(spread(cell, [one[0:1], one[2:3]]))
    for two in other:
        cell = two[1:2].astype(jnp.int32)
        low_a.append(hot_rows(cell, halo - rows, halo_index))
        low_b.append(spread(cell, [two[0:1]]))
    for two in other:
        cell = two[3:4].astype(jnp.int32)
        high_a.append(hot_rows(cell, 0, halo_index))
        high_b.append(spread(cell, [two[2:3]]))

    group = LANES // EDGE
    edge_parts = []
    for g in range(-(-devices // group)):
        total = got[g * group]
        for i in range(g * group + 1, min(devices, (g + 1) * group)):
            total = total + got[i]
        edge_parts.append(total)
    edge = jnp.concatenate(edge_parts, axis=1)
    width = edge.shape[1]
    spot = iota((8, width), 1)
    e = spot % EDGE
    count = edge[7:8]
    missing = jnp.zeros((8, width), jnp.float32)
    for reach in range(-SW, SW + 1):
        if reach == 0:
            continue
        if reach < 0:
            crosses = (e < -reach) & (spot >= -reach)
        else:
            crosses = (e >= EDGE - reach) & (spot < width - reach)
        keep = crosses & (count >= float(abs(reach)))
        missing = missing + jnp.where(
            keep,
            line_taps[0:1, reach + SW : reach + SW + 1] * pltpu.roll(edge, (-reach) % width, 1),
            0.0,
        )
    edge_cell = edge[6:7].astype(jnp.int32) - me * block
    edge_row = jnp.clip(edge_cell >> shift, -2 * rows, 2 * rows)
    for g in range(width // LANES):
        at = slice(g * LANES, (g + 1) * LANES)
        b = spread(edge_cell[:, at], [missing[4:5, at], missing[5:6, at]])
        own_a.append(hot16(row_index, edge_row[:, at]))
        own_b.append(b)
        low_a.append(hot16(halo_index, edge_row[:, at] + halo))
        low_b.append(b[: 2 * LANES])
        high_a.append(hot16(halo_index, edge_row[:, at] - rows))
        high_b.append(b[: 2 * LANES])

    zeros = jnp.zeros((field.shape[0], PAD, lanes), jnp.float32)
    field[:, 0:PAD, :] = zeros
    field[:, PAD + size_y :, :] = zeros
    inside = slice(PAD, PAD + size_y)
    top = REACH + size_x

    out = inject(own_a, own_b)
    low_out = inject(low_a, low_b)
    high_out = inject(high_a, high_b)
    first = (out[:, 0:lanes] + out[:, lanes : 2 * lanes]).reshape(size_x, size_y, lanes)
    source1[...] = (out[:, 2 * lanes : 3 * lanes] + out[:, 3 * lanes :]).reshape(
        size_x, size_y, lanes
    )
    field[REACH:top, inside, :] = free[REACH:top] + scale[REACH:top] * first
    done = [
        pltpu.make_async_copy(field.at[REACH:top, inside, :], prior_far, out_sems.at[0])
    ]
    done[0].start()
    first = (low_out[:, 0:lanes] + low_out[:, lanes:]).reshape(REACH, size_y, lanes)
    field[0:REACH, inside, :] = free[0:REACH] + scale[0:REACH] * first
    first = (high_out[:, 0:lanes] + high_out[:, lanes:]).reshape(REACH, size_y, lanes)
    field[top:, inside, :] = free[top:] + scale[top:] * first

    half = size_x // 2
    for part in range(2):
        planes = slice(part * half, (part + 1) * half)

        for x in range(part * half, (part + 1) * half):
            at = x + REACH
            fresh = field[at, inside, :]
            following = (
                2.0 * fresh
                - now[x]
                + scale[at] * (laplacian_plane(field, at, size_y) + source1[x])
            )
            last[x] = following
            gradient[x] = weight0[x] * fresh + weight1[x] * following

        done += started(
            out_sems.at[pl.ds(1 + 2 * part, 2)],
            (last.at[planes], last_far.at[planes]),
            (gradient.at[planes], gradient_far.at[planes]),
        )
    for copy in done:
        copy.wait()


def body(
    synthetic,
    observed,
    offsets,
    lines,
    owners,
    cells,
    taps,
    line_taps,
    velocity,
    adjoint_old,
    adjoint_now,
    forward,
):
    count = synthetic.shape[0]
    size_x, size_y, lanes = velocity.shape
    devices = lax.axis_size("sub")
    cap = max(2, 2 * count // devices)
    f32 = jnp.float32

    pair = [(i, i ^ 1) for i in range(devices)]
    following = [(i, i + 1) for i in range(1, devices - 1, 2)]
    following = following + [(b, a) for a, b in following]

    plane = (size_y, lanes)
    outer = size_x + 2 * REACH
    inner = pltpu.VMEM((size_x,) + plane, f32)
    padded = pltpu.VMEM((outer, size_y + 2 * PAD, lanes), f32)
    halo = pltpu.VMEM((3 * REACH,) + plane, f32)
    wider = pltpu.VMEM((outer,) + plane, f32)
    inner_far = pltpu.HBM((size_x,) + plane, f32)
    wider_far = pltpu.HBM((outer,) + plane, f32)
    dma = pltpu.SemaphoreType.DMA

    row = (1, count)
    small = pltpu.VMEM(row, jnp.int32)
    traces = pltpu.VMEM(synthetic.shape, f32)
    send, to_pair, to_next = pl.pallas_call(
        functools.partial(send_kernel, devices, cap, velocity.size),
        out_shape=(pltpu.HBM((devices, 8, LANES), f32), halo, halo),
        in_specs=[FAR] * 11,
        out_specs=(FAR, VMEM, VMEM),
        scratch_shapes=[
            small,
            small,
            pltpu.VMEM((1, taps.shape[0]), f32),
            small,
            pltpu.VMEM(lines.shape, jnp.int32),
            pltpu.VMEM((1, line_taps.shape[0]), f32),
            traces,
            traces,
            inner,
            inner,
            padded,
            pltpu.VMEM((devices, 8, LANES), f32),
            dma((12,)),
        ],
        compiler_params=PARAMS,
        name="send",
    )(
        *far(
            owners.reshape(row),
            cells.reshape(row),
            taps.reshape(1, -1),
            offsets.reshape(row),
            lines,
            line_taps.reshape(1, -1),
            synthetic,
            observed,
            adjoint_now,
            velocity,
            adjoint_old,
        )
    )
    from_next = lax.ppermute(to_next, "sub", following)
    from_pair = lax.ppermute(to_pair, "sub", pair)
    got = lax.all_to_all(send, "sub", split_axis=0, concat_axis=0, tiled=True)

    partial, now, vel, weight0, weight1, line_row = pl.pallas_call(
        inner_kernel,
        out_shape=(inner,) * 5 + (pltpu.VMEM((1, line_taps.shape[0]), f32),),
        in_specs=[FAR] * 5,
        out_specs=(VMEM,) * 6,
        scratch_shapes=[padded, inner, pltpu.VMEM(forward.shape, f32), dma((5,))],
        compiler_params=PARAMS,
        name="inner",
    )(*far(adjoint_old, adjoint_now, velocity, forward, line_taps.reshape(1, -1)))
    free, scale = pl.pallas_call(
        first_kernel,
        out_shape=(wider,) * 2,
        in_specs=[VMEM] * 5,
        out_specs=(VMEM,) * 2,
        compiler_params=PARAMS,
        name="first",
    )(near(from_pair), near(from_next), near(partial), near(now), near(vel))

    field = jax.ShapeDtypeStruct((size_x,) + plane, f32)
    return pl.pallas_call(
        functools.partial(second_kernel, devices, cap),
        out_shape=(field, field, field),
        in_specs=[VMEM] * 7,
        out_specs=(FAR,) * 3,
        scratch_shapes=[
            inner,
            inner,
            pltpu.VMEM((outer, size_y + 2 * PAD, lanes), f32),
            inner,
            dma((5,)),
        ],
        compiler_params=PARAMS,
        name="second",
    )(
        near(got),
        near(free),
        near(scale),
        near(now),
        near(weight0),
        near(weight1),
        near(line_row),
    )


def solution(mesh):
    return jax.shard_map(
        body,
        mesh=mesh,
        in_specs=(
            P(("shot", "sub"), None),
            P(("shot", "sub"), None),
            P(("shot", "sub")),
            P(None, ("shot", "sub")),
            P(("shot", "sub"), None),
            P(("shot", "sub")),
            P(),
            P(),
            P("sub", None, None),
            P(("shot", "sub"), None, None),
            P(("shot", "sub"), None, None),
            P(None, ("shot", "sub"), None, None),
        ),
        out_specs=(
            P(("shot", "sub"), None, None),
            P(("shot", "sub"), None, None),
            P(("shot", "sub"), None, None),
        ),
        check_vma=False,
    )
```

```python
import functools

import jax
import jax.numpy as jnp
from jax import lax
from jax.experimental import pallas as pl
from jax.experimental.pallas import tpu as pltpu
from jax.sharding import PartitionSpec as P

SW = 4
STEPS = 2
REACH = 4
LANES = 128
EDGE = 2 * SW

COEF = (-205.0 / 72.0, 8.0 / 5.0, -1.0 / 5.0, 8.0 / 315.0, -1.0 / 560.0)
DT_OVER_H = 0.18

VMEM = pl.BlockSpec(memory_space=pltpu.VMEM)
FAR = pl.BlockSpec(memory_space=pltpu.HBM)
PARAMS = pltpu.CompilerParams(vmem_limit_bytes=16 * 2**20)
NT_DIMS = (((1,), (1,)), ((), ()))


def near(array):
    return pltpu.with_memory_space_constraint(array, pltpu.VMEM)


def far(*arrays):
    return [pltpu.with_memory_space_constraint(array, pltpu.HBM) for array in arrays]


def started(sems, *pairs):
    copies = [
        pltpu.make_async_copy(source, target, sems.at[i])
        for i, (source, target) in enumerate(pairs)
    ]
    for copy in copies:
        copy.start()
    return copies


def parts_of(value, count):
    parts = []
    for _ in range(count):
        part = value.astype(jnp.bfloat16).astype(jnp.float32)
        parts.append(part)
        value = value - part
    return parts


def iota(shape, axis):
    return lax.broadcasted_iota(jnp.int32, shape, axis)


PACKED = 16


def across16(row):
    return jnp.broadcast_to(row, (PACKED, row.shape[1])).astype(jnp.int16)[None]


def index16(count, width):
    rows = iota((count, width), 0).astype(jnp.int16)
    return rows.reshape(count // PACKED, PACKED, width)


def same16(index, row):
    return index == across16(row)


def pick16(mask, row):
    width = row.shape[1]
    wide = jnp.broadcast_to(row, (PACKED, width)).astype(jnp.bfloat16)
    picked = jnp.where(mask, wide[None], jnp.zeros((), jnp.bfloat16))
    return picked.reshape(-1, width)


def hot16(index, row):
    return pick16(same16(index, row), jnp.ones(row.shape, jnp.float32))


PAD = 8


def laplacian_plane(field, x, size_y):
    centre = field[x, PAD : PAD + size_y, :]
    lanes = centre.shape[1]
    lane = iota(centre.shape, 1)
    total = 3.0 * COEF[0] * centre
    for k in range(1, 5):
        near = field[x + k, PAD : PAD + size_y, :] + field[x - k, PAD : PAD + size_y, :]
        near = near + field[x, PAD + k : PAD + k + size_y, :]
        near = near + field[x, PAD - k : PAD - k + size_y, :]
        near = near + jnp.where(lane < lanes - k, pltpu.roll(centre, lanes - k, 1), 0.0)
        near = near + jnp.where(lane >= k, pltpu.roll(centre, k, 1), 0.0)
        total = total + COEF[k] * near
    return total


def squared(speed):
    factor = DT_OVER_H * speed
    return factor * factor


def send_kernel(
    devices,
    place_of,
    cap,
    block,
    own_far,
    cells_far,
    taps_far,
    off_far,
    lines_far,
    line_taps_far,
    syn_far,
    obs_far,
    now_far,
    vel_far,
    old_far,
    send_far,
    to_pair,
    to_next,
    own,
    cells,
    taps,
    off,
    lines,
    line_taps,
    syn,
    obs,
    old,
    vel,
    wide,
    send,
    sems,
):
    size_x, size_y, lanes = old.shape
    inside = slice(PAD, PAD + size_y)
    copies = started(
        sems,
        (own_far, own),
        (taps_far, taps),
        (syn_far, syn),
        (obs_far, obs),
        (cells_far, cells),
        (off_far, off),
        (lines_far, lines),
        (line_taps_far, line_taps),
        (now_far, wide.at[REACH : REACH + size_x, inside, :]),
        (vel_far, vel),
        (old_far, old),
    )
    edge = jnp.zeros((wide.shape[0], PAD, lanes), jnp.float32)
    wide[:, 0:PAD, :] = edge
    wide[:, PAD + size_y :, :] = edge
    blank = jnp.zeros((REACH, size_y, lanes), jnp.float32)
    wide[0:REACH, inside, :] = blank
    wide[REACH + size_x :, inside, :] = blank
    for copy in copies[:2]:
        copy.wait()
    me = lax.axis_index("sub")
    count, samples = syn.shape
    ntap = taps.shape[1]
    pack = LANES // cap
    group = LANES // EDGE
    place = iota((1, count), 1)
    owner = own[...]
    owned = same16(index16(devices, count), owner)
    one_hot = pick16(owned, jnp.ones((1, count), jnp.float32))
    chunks = [one_hot[:, at : at + LANES] for at in range(0, count, LANES)]
    ahead = index16(LANES, LANES) < across16(iota((1, LANES), 1))
    ranks = jnp.dot(
        jnp.concatenate(chunks, axis=0),
        pick16(ahead, jnp.ones((1, LANES), jnp.float32)),
        preferred_element_type=jnp.float32,
    )
    base = jnp.zeros((devices, 1), jnp.float32)
    rank = []
    for i, chunk in enumerate(chunks):
        chunk = chunk.astype(jnp.float32)
        rank.append(
            jnp.sum(
                chunk * (ranks[i * devices : (i + 1) * devices] + base), axis=0, keepdims=True
            )
        )
        base = base + jnp.sum(chunk, axis=1, keepdims=True)
    rank = jnp.concatenate(rank, axis=1).astype(jnp.int32)
    lane = index16(LANES, count)
    slot = hot16(lane, rank + (me % pack) * cap)
    edge_lane = jnp.where(
        place < SW, place, jnp.where(place >= count - SW, place - count + EDGE, -LANES)
    )
    chosen = hot16(lane, edge_lane + (me % group) * EDGE)

    row = jnp.concatenate([taps[...], jnp.zeros((1, samples - ntap), jnp.float32)], axis=1)
    starts = -(-(samples - ntap + 1) // 16) * 16
    toeplitz = pltpu.roll(
        jnp.broadcast_to(row, (starts, samples)), 0, 1, stride=1, stride_axis=0
    )
    for copy in copies[2:-3]:
        copy.wait()
    residual = syn[...] - obs[...]
    r_high = residual.astype(jnp.bfloat16)
    r_low = (residual - r_high.astype(jnp.float32)).astype(jnp.bfloat16)
    t_high = toeplitz.astype(jnp.bfloat16)
    t_low = (toeplitz - t_high.astype(jnp.float32)).astype(jnp.bfloat16)
    all_starts = sum(
        lax.dot_general(a, b, NT_DIMS, preferred_element_type=jnp.float32)
        for a, b in ((t_high, r_low), (t_low, r_high), (t_high, r_high))
    )
    start = iota((starts, count), 0)
    offset = off[...]
    filtered = [
        jnp.sum(jnp.where(start == offset + step, all_starts, 0.0), axis=0, keepdims=True)
        for step in range(STEPS)
    ]
    both = jnp.concatenate(filtered + [jnp.zeros((8 - STEPS, count), jnp.float32)], axis=0)
    before = lines[0:1, :]
    after = lines[1:2, :]
    sources = jnp.zeros((8, count), jnp.float32)
    for reach in range(-SW, SW + 1):
        term = line_taps[0:1, reach + SW : reach + SW + 1] * (
            pltpu.roll(both, (-reach) % count, 1) if reach else both
        )
        if reach < 0:
            keep = (before >= -reach) & (place >= -reach)
        elif reach > 0:
            keep = (after >= reach) & (place < count - reach)
        else:
            keep = before >= 0
        sources = sources + jnp.where(keep, term, 0.0)
    cell = cells[...]
    high = (cell >> 8).astype(jnp.float32)
    low = (cell & 255).astype(jnp.float32)
    pieces = parts_of(sources[0:1], 3) + parts_of(sources[1:2], 3) + [high, low]
    spread = jnp.concatenate([pick16(owned, piece) for piece in pieces], axis=0)
    out = lax.dot_general(spread, slot, NT_DIMS, preferred_element_type=jnp.float32)
    part = [out[k * devices : (k + 1) * devices] for k in range(8)]
    value0 = part[0] + part[1] + part[2]
    value1 = part[3] + part[4] + part[5]
    where = 256.0 * part[6] + part[7]
    none = jnp.zeros((1, LANES), jnp.float32)

    def to_upper(rows):
        return pltpu.roll(jnp.concatenate([none, rows[:-1]], axis=0), LANES // 2, 1)

    def to_lower(rows):
        return pltpu.roll(jnp.concatenate([rows[1:], none], axis=0), LANES // 2, 1)

    def put(k, rows):
        for to, at in enumerate(place_of):
            send[at, k : k + 1, :] = rows[to : to + 1]

    put(0, value0 + to_upper(value0))
    put(1, where + to_upper(where))
    put(2, value1 + to_lower(value0))
    put(3, to_lower(where))
    count_ = jnp.where(place < SW, before, after).astype(jnp.float32)
    edge_rows = (
        parts_of(both[0:1], 3)
        + parts_of(both[1:2], 3)
        + [owner.astype(jnp.float32), high, low, count_]
    )
    edge_rows = jnp.concatenate(
        edge_rows + [jnp.zeros((16 - len(edge_rows), count), jnp.float32)], axis=0
    ).astype(jnp.bfloat16)
    edge = lax.dot_general(edge_rows, chosen, NT_DIMS, preferred_element_type=jnp.float32)
    edge_cell = edge[6:7] * float(block) + 256.0 * edge[7:8] + edge[8:9]
    shape = (devices, LANES)
    put(4, jnp.broadcast_to(edge[0:1] + edge[1:2] + edge[2:3], shape))
    put(5, jnp.broadcast_to(edge[3:4] + edge[4:5] + edge[5:6], shape))
    put(6, jnp.broadcast_to(edge_cell, shape))
    put(7, jnp.broadcast_to(edge[9:10], shape))
    sent = pltpu.make_async_copy(send, send_far, sems.at[len(copies)])
    sent.start()
    for copy in copies[-3:]:
        copy.wait()
    odd = me % 2

    def half(target, start):
        for i in range(REACH):
            x = start + i
            own_now = wide[REACH + x, inside, :]
            speed = vel[x]
            target[i] = own_now
            target[REACH + i] = (
                2.0 * own_now
                - old[x]
                + squared(speed) * laplacian_plane(wide, x + REACH, size_y)
            )
            target[2 * REACH + i] = speed

    far_half = size_x - REACH
    half(to_next, far_half * odd)
    half(to_pair, far_half * (1 - odd))
    sent.wait()


def inner_kernel(
    old_far,
    now_far,
    vel_far,
    fwd_far,
    line_taps_far,
    partial,
    now,
    vel,
    weight0,
    weight1,
    line_taps,
    wide,
    old,
    fwd,
    sems,
):
    size_x, size_y, lanes = old.shape
    inside = slice(PAD, PAD + size_y)
    copies = started(
        sems,
        (now_far, wide.at[REACH : REACH + size_x, inside, :]),
        (vel_far, vel),
        (old_far, old),
        (fwd_far, fwd),
        (line_taps_far, line_taps),
    )
    edge = jnp.zeros((wide.shape[0], PAD, lanes), jnp.float32)
    wide[:, 0:PAD, :] = edge
    wide[:, PAD + size_y :, :] = edge
    blank = jnp.zeros((REACH, size_y, lanes), jnp.float32)
    wide[0:REACH, inside, :] = blank
    wide[REACH + size_x :, inside, :] = blank
    for copy in copies:
        copy.wait()

    for x in range(size_x):
        speed = vel[x]
        now[x] = wide[REACH + x, inside, :]
        partial[x] = (
            2.0 * now[x]
            - old[x]
            + squared(speed) * laplacian_plane(wide, x + REACH, size_y)
        )
        weight = 2.0 / (speed * speed * speed)
        f1 = fwd[1, x]
        f2 = fwd[2, x]
        weight0[x] = weight * (fwd[0, x] - 2.0 * f1 + f2)
        weight1[x] = weight * (f1 - 2.0 * f2 + fwd[3, x])


def across(field, x, low, high):
    total = None
    for k in range(1, 5):
        for at in (x - k, x + k):
            if low <= at < high:
                term = COEF[k] * field[at - low]
                total = term if total is None else total + term
    return total


def first_kernel(
    from_pair, from_next, partial, now, vel, free, scale
):
    odd = lax.axis_index("sub") % 2
    size_x = now.shape[0]
    top = REACH + size_x

    def border(source, first_out, low):
        for i in range(REACH):
            factor = squared(source[2 * REACH + i])
            scale[first_out + i] = factor
            free[first_out + i] = source[REACH + i] + factor * across(now, low + i, 0, size_x)
        planes = range(REACH) if low < 0 else range(size_x - REACH, size_x)
        for x in planes:
            factor = squared(vel[x])
            scale[REACH + x] = factor
            free[REACH + x] = partial[x] + factor * across(source, x, low, low + REACH)

    @pl.when(odd == 0)
    def _():
        border(from_next, 0, -REACH)
        border(from_pair, top, size_x)

    @pl.when(odd == 1)
    def _():
        border(from_pair, 0, -REACH)
        border(from_next, top, size_x)


def second_kernel(
    devices,
    place_of,
    cap,
    got,
    free,
    scale,
    now,
    weight0,
    weight1,
    line_taps,
    prior_far,
    last_far,
    gradient_far,
    last,
    gradient,
    field,
    source1,
    out_sems,
):
    me = lax.axis_index("sub")
    size_x, size_y, lanes = now.shape
    rows = size_x * size_y
    halo = REACH * size_y
    block = rows * lanes
    pack = LANES // cap
    lane8 = iota((8, LANES), 1)
    shift = lanes.bit_length() - 1

    def hot_rows(cell, move, index):
        return hot16(index, (cell >> shift) + move)

    def spread(cell, values):
        at = same16(zs, cell & (lanes - 1))
        stack = []
        for value in values:
            for part in parts_of(value, 2):
                stack.append(pick16(at, part))
        return jnp.concatenate(stack, axis=0)

    def inject(a, b):
        return lax.dot_general(
            jnp.concatenate(a, axis=1),
            jnp.concatenate(b, axis=1),
            NT_DIMS,
            preferred_element_type=jnp.float32,
        )

    zs = index16(LANES, LANES)
    row_index = index16(rows, LANES)
    halo_index = index16(halo, LANES)

    own_a, own_b, low_a, low_b, high_a, high_b = [], [], [], [], [], []
    mine, other = [], []
    for g in range(devices // pack):
        tiles = [got[place_of[g * pack + q]] for q in range(pack)]
        one, two = tiles[0], tiles[pack // 2]
        for q in range(1, pack):
            later = lane8 >= q * cap
            one = jnp.where(later, tiles[q], one)
            two = jnp.where(later, tiles[(q + pack // 2) % pack], two)
        mine.append(one)
        other.append(two)
    for one in mine:
        cell = one[1:2].astype(jnp.int32)
        own_a.append(hot_rows(cell, 0, row_index))
        own_b.append(spread(cell, [one[0:1], one[2:3]]))
    for two in other:
        cell = two[1:2].astype(jnp.int32)
        low_a.append(hot_rows(cell, halo - rows, halo_index))
        low_b.append(spread(cell, [two[0:1]]))
    for two in other:
        cell = two[3:4].astype(jnp.int32)
        high_a.append(hot_rows(cell, 0, halo_index))
        high_b.append(spread(cell, [two[2:3]]))

    group = LANES // EDGE
    edge_parts = []
    for g in range(-(-devices // group)):
        total = got[place_of[g * group]]
        for i in range(g * group + 1, min(devices, (g + 1) * group)):
            total = total + got[place_of[i]]
        edge_parts.append(total)
    edge = jnp.concatenate(edge_parts, axis=1)
    width = edge.shape[1]
    spot = iota((8, width), 1)
    e = spot % EDGE
    count = edge[7:8]
    missing = jnp.zeros((8, width), jnp.float32)
    for reach in range(-SW, SW + 1):
        if reach == 0:
            continue
        if reach < 0:
            crosses = (e < -reach) & (spot >= -reach)
        else:
            crosses = (e >= EDGE - reach) & (spot < width - reach)
        keep = crosses & (count >= float(abs(reach)))
        missing = missing + jnp.where(
            keep,
            line_taps[0:1, reach + SW : reach + SW + 1] * pltpu.roll(edge, (-reach) % width, 1),
            0.0,
        )
    edge_cell = edge[6:7].astype(jnp.int32) - me * block
    edge_row = jnp.clip(edge_cell >> shift, -2 * rows, 2 * rows)
    for g in range(width // LANES):
        at = slice(g * LANES, (g + 1) * LANES)
        b = spread(edge_cell[:, at], [missing[4:5, at], missing[5:6, at]])
        own_a.append(hot16(row_index, edge_row[:, at]))
        own_b.append(b)
        low_a.append(hot16(halo_index, edge_row[:, at] + halo))
        low_b.append(b[: 2 * LANES])
        high_a.append(hot16(halo_index, edge_row[:, at] - rows))
        high_b.append(b[: 2 * LANES])

    zeros = jnp.zeros((field.shape[0], PAD, lanes), jnp.float32)
    field[:, 0:PAD, :] = zeros
    field[:, PAD + size_y :, :] = zeros
    inside = slice(PAD, PAD + size_y)
    top = REACH + size_x

    out = inject(own_a, own_b)
    low_out = inject(low_a, low_b)
    high_out = inject(high_a, high_b)
    first = (out[:, 0:lanes] + out[:, lanes : 2 * lanes]).reshape(size_x, size_y, lanes)
    source1[...] = (out[:, 2 * lanes : 3 * lanes] + out[:, 3 * lanes :]).reshape(
        size_x, size_y, lanes
    )
    field[REACH:top, inside, :] = free[REACH:top] + scale[REACH:top] * first
    done = [
        pltpu.make_async_copy(field.at[REACH:top, inside, :], prior_far, out_sems.at[0])
    ]
    done[0].start()
    first = (low_out[:, 0:lanes] + low_out[:, lanes:]).reshape(REACH, size_y, lanes)
    field[0:REACH, inside, :] = free[0:REACH] + scale[0:REACH] * first
    first = (high_out[:, 0:lanes] + high_out[:, lanes:]).reshape(REACH, size_y, lanes)
    field[top:, inside, :] = free[top:] + scale[top:] * first

    half = size_x // 2
    for part in range(2):
        planes = slice(part * half, (part + 1) * half)

        for x in range(part * half, (part + 1) * half):
            at = x + REACH
            fresh = field[at, inside, :]
            following = (
                2.0 * fresh
                - now[x]
                + scale[at] * (laplacian_plane(field, at, size_y) + source1[x])
            )
            last[x] = following
            gradient[x] = weight0[x] * fresh + weight1[x] * following

        done += started(
            out_sems.at[pl.ds(1 + 2 * part, 2)],
            (last.at[planes], last_far.at[planes]),
            (gradient.at[planes], gradient_far.at[planes]),
        )
    for copy in done:
        copy.wait()


def body(
    synthetic,
    observed,
    offsets,
    lines,
    owners,
    cells,
    taps,
    line_taps,
    velocity,
    adjoint_old,
    adjoint_now,
    forward,
):
    count = synthetic.shape[0]
    size_x, size_y, lanes = velocity.shape
    devices = lax.axis_size("sub")
    cap = max(2, 2 * count // devices)
    f32 = jnp.float32

    order = list(range(devices))[::-1]
    place_of = [order.index(i) for i in range(devices)]
    pair = [(i, i ^ 1) for i in range(devices)]
    following = [(i, i + 1) for i in range(1, devices - 1, 2)]
    following = following + [(b, a) for a, b in following]

    plane = (size_y, lanes)
    outer = size_x + 2 * REACH
    inner = pltpu.VMEM((size_x,) + plane, f32)
    padded = pltpu.VMEM((outer, size_y + 2 * PAD, lanes), f32)
    halo = pltpu.VMEM((3 * REACH,) + plane, f32)
    wider = pltpu.VMEM((outer,) + plane, f32)
    inner_far = pltpu.HBM((size_x,) + plane, f32)
    wider_far = pltpu.HBM((outer,) + plane, f32)
    dma = pltpu.SemaphoreType.DMA

    row = (1, count)
    small = pltpu.VMEM(row, jnp.int32)
    traces = pltpu.VMEM(synthetic.shape, f32)
    send, to_pair, to_next = pl.pallas_call(
        functools.partial(send_kernel, devices, place_of, cap, velocity.size),
        out_shape=(pltpu.HBM((devices, 8, LANES), f32), halo, halo),
        in_specs=[FAR] * 11,
        out_specs=(FAR, VMEM, VMEM),
        scratch_shapes=[
            small,
            small,
            pltpu.VMEM((1, taps.shape[0]), f32),
            small,
            pltpu.VMEM(lines.shape, jnp.int32),
            pltpu.VMEM((1, line_taps.shape[0]), f32),
            traces,
            traces,
            inner,
            inner,
            padded,
            pltpu.VMEM((devices, 8, LANES), f32),
            dma((12,)),
        ],
        compiler_params=PARAMS,
        name="send",
    )(
        *far(
            owners.reshape(row),
            cells.reshape(row),
            taps.reshape(1, -1),
            offsets.reshape(row),
            lines,
            line_taps.reshape(1, -1),
            synthetic,
            observed,
            adjoint_now,
            velocity,
            adjoint_old,
        )
    )
    from_next = lax.ppermute(to_next, "sub", following)
    from_pair = lax.ppermute(to_pair, "sub", pair)
    got = lax.all_to_all(
        send, "sub", split_axis=0, concat_axis=0, axis_index_groups=[order], tiled=True
    )

    partial, now, vel, weight0, weight1, line_row = pl.pallas_call(
        inner_kernel,
        out_shape=(inner,) * 5 + (pltpu.VMEM((1, line_taps.shape[0]), f32),),
        in_specs=[FAR] * 5,
        out_specs=(VMEM,) * 6,
        scratch_shapes=[padded, inner, pltpu.VMEM(forward.shape, f32), dma((5,))],
        compiler_params=PARAMS,
        name="inner",
    )(*far(adjoint_old, adjoint_now, velocity, forward, line_taps.reshape(1, -1)))
    free, scale = pl.pallas_call(
        first_kernel,
        out_shape=(wider,) * 2,
        in_specs=[VMEM] * 5,
        out_specs=(VMEM,) * 2,
        compiler_params=PARAMS,
        name="first",
    )(near(from_pair), near(from_next), near(partial), near(now), near(vel))

    field = jax.ShapeDtypeStruct((size_x,) + plane, f32)
    return pl.pallas_call(
        functools.partial(second_kernel, devices, place_of, cap),
        out_shape=(field, field, field),
        in_specs=[VMEM] * 7,
        out_specs=(FAR,) * 3,
        scratch_shapes=[
            inner,
            inner,
            pltpu.VMEM((outer, size_y + 2 * PAD, lanes), f32),
            inner,
            dma((5,)),
        ],
        compiler_params=PARAMS,
        name="second",
    )(
        near(got),
        near(free),
        near(scale),
        near(now),
        near(weight0),
        near(weight1),
        near(line_row),
    )


def solution(mesh):
    return jax.shard_map(
        body,
        mesh=mesh,
        in_specs=(
            P(("shot", "sub"), None),
            P(("shot", "sub"), None),
            P(("shot", "sub")),
            P(None, ("shot", "sub")),
            P(("shot", "sub"), None),
            P(("shot", "sub")),
            P(),
            P(),
            P("sub", None, None),
            P(("shot", "sub"), None, None),
            P(("shot", "sub"), None, None),
            P(None, ("shot", "sub"), None, None),
        ),
        out_specs=(
            P(("shot", "sub"), None, None),
            P(("shot", "sub"), None, None),
            P(("shot", "sub"), None, None),
        ),
        check_vma=False,
    )
```

```python
import functools

import jax
import jax.numpy as jnp
from jax import lax
from jax.experimental import pallas as pl
from jax.experimental.pallas import tpu as pltpu
from jax.sharding import PartitionSpec as P

SW = 4
STEPS = 2
REACH = 4
LANES = 128
EDGE = 2 * SW

COEF = (-205.0 / 72.0, 8.0 / 5.0, -1.0 / 5.0, 8.0 / 315.0, -1.0 / 560.0)
DT_OVER_H = 0.18

VMEM = pl.BlockSpec(memory_space=pltpu.VMEM)
FAR = pl.BlockSpec(memory_space=pltpu.HBM)
PARAMS = pltpu.CompilerParams(vmem_limit_bytes=16 * 2**20)
NT_DIMS = (((1,), (1,)), ((), ()))


def near(array):
    return pltpu.with_memory_space_constraint(array, pltpu.VMEM)


def far(*arrays):
    return [pltpu.with_memory_space_constraint(array, pltpu.HBM) for array in arrays]


def started(sems, *pairs):
    copies = [
        pltpu.make_async_copy(source, target, sems.at[i])
        for i, (source, target) in enumerate(pairs)
    ]
    for copy in copies:
        copy.start()
    return copies


def parts_of(value, count):
    parts = []
    for _ in range(count):
        part = value.astype(jnp.bfloat16).astype(jnp.float32)
        parts.append(part)
        value = value - part
    return parts


def iota(shape, axis):
    return lax.broadcasted_iota(jnp.int32, shape, axis)


PACKED = 16


def across16(row):
    return jnp.broadcast_to(row, (PACKED, row.shape[1])).astype(jnp.int16)[None]


def index16(count, width):
    rows = iota((count, width), 0).astype(jnp.int16)
    return rows.reshape(count // PACKED, PACKED, width)


def same16(index, row):
    return index == across16(row)


def pick16(mask, row):
    width = row.shape[1]
    wide = jnp.broadcast_to(row, (PACKED, width)).astype(jnp.bfloat16)
    picked = jnp.where(mask, wide[None], jnp.zeros((), jnp.bfloat16))
    return picked.reshape(-1, width)


def hot16(index, row):
    return pick16(same16(index, row), jnp.ones(row.shape, jnp.float32))


PAD = 8


class Planes:
    def __init__(self, rows, height):
        self.rows, self.height = rows, height

    def __getitem__(self, i):
        return self.rows[i * self.height : (i + 1) * self.height, :]

    def __setitem__(self, i, value):
        self.rows[i * self.height : (i + 1) * self.height, :] = value


def laplacian_plane(field, x, size_y):
    centre = field[x, PAD : PAD + size_y, :]
    lanes = centre.shape[1]
    lane = iota(centre.shape, 1)
    total = 3.0 * COEF[0] * centre
    for k in range(1, 5):
        near = field[x + k, PAD : PAD + size_y, :] + field[x - k, PAD : PAD + size_y, :]
        near = near + field[x, PAD + k : PAD + k + size_y, :]
        near = near + field[x, PAD - k : PAD - k + size_y, :]
        near = near + jnp.where(lane < lanes - k, pltpu.roll(centre, lanes - k, 1), 0.0)
        near = near + jnp.where(lane >= k, pltpu.roll(centre, k, 1), 0.0)
        total = total + COEF[k] * near
    return total


def squared(speed):
    factor = DT_OVER_H * speed
    return factor * factor


def half_block(target, start, wide, vel, old):
    size_y = old.shape[1]
    inside = slice(PAD, PAD + size_y)
    for i in range(REACH):
        x = start + i
        own_now = wide[REACH + x, inside, :]
        speed = vel[x]
        target[i] = own_now
        target[REACH + i] = (
            2.0 * own_now
            - old[x]
            + squared(speed) * laplacian_plane(wide, x + REACH, size_y)
        )
        target[2 * REACH + i] = speed


def next_kernel(
    now_far,
    vel_far,
    old_far,
    own_far,
    cells_far,
    taps_far,
    off_far,
    lines_far,
    line_taps_far,
    syn_far,
    obs_far,
    to_next,
    wide,
    vel,
    old,
    own,
    cells,
    taps,
    off,
    lines,
    line_taps,
    syn,
    obs,
    sems,
):
    size_x, size_y, lanes = old.shape
    inside = slice(PAD, PAD + size_y)
    copies = started(
        sems,
        (now_far, wide.at[REACH : REACH + size_x, inside, :]),
        (vel_far, vel),
        (old_far, old),
        (own_far, own),
        (cells_far, cells),
        (taps_far, taps),
        (off_far, off),
        (lines_far, lines),
        (line_taps_far, line_taps),
        (syn_far, syn),
        (obs_far, obs),
    )
    edge = jnp.zeros((wide.shape[0], PAD, lanes), jnp.float32)
    wide[:, 0:PAD, :] = edge
    wide[:, PAD + size_y :, :] = edge
    blank = jnp.zeros((REACH, size_y, lanes), jnp.float32)
    wide[0:REACH, inside, :] = blank
    wide[REACH + size_x :, inside, :] = blank
    for copy in copies[:3]:
        copy.wait()
    odd = lax.axis_index("sub") % 2
    used = 3 * REACH * size_y
    to_next[used:, :] = jnp.zeros((to_next.shape[0] - used, lanes), jnp.float32)
    half_block(Planes(to_next, size_y), (size_x - REACH) * odd, wide, vel, old)
    for copy in copies[3:]:
        copy.wait()


def send_kernel(
    devices,
    place_of,
    cap,
    block,
    wide,
    vel,
    old,
    own,
    cells,
    taps,
    off,
    lines,
    line_taps,
    syn,
    obs,
    send_far,
    to_pair,
    send,
    sems,
):
    me = lax.axis_index("sub")
    count, samples = syn.shape
    ntap = taps.shape[1]
    pack = LANES // cap
    group = LANES // EDGE
    place = iota((1, count), 1)
    owner = own[...]
    owned = same16(index16(devices, count), owner)
    one_hot = pick16(owned, jnp.ones((1, count), jnp.float32))
    chunks = [one_hot[:, at : at + LANES] for at in range(0, count, LANES)]
    ahead = index16(LANES, LANES) < across16(iota((1, LANES), 1))
    ranks = jnp.dot(
        jnp.concatenate(chunks, axis=0),
        pick16(ahead, jnp.ones((1, LANES), jnp.float32)),
        preferred_element_type=jnp.float32,
    )
    base = jnp.zeros((devices, 1), jnp.float32)
    rank = []
    for i, chunk in enumerate(chunks):
        chunk = chunk.astype(jnp.float32)
        rank.append(
            jnp.sum(
                chunk * (ranks[i * devices : (i + 1) * devices] + base), axis=0, keepdims=True
            )
        )
        base = base + jnp.sum(chunk, axis=1, keepdims=True)
    rank = jnp.concatenate(rank, axis=1).astype(jnp.int32)
    lane = index16(LANES, count)
    slot = hot16(lane, rank + (me % pack) * cap)
    edge_lane = jnp.where(
        place < SW, place, jnp.where(place >= count - SW, place - count + EDGE, -LANES)
    )
    chosen = hot16(lane, edge_lane + (me % group) * EDGE)

    row = jnp.concatenate([taps[...], jnp.zeros((1, samples - ntap), jnp.float32)], axis=1)
    starts = -(-(samples - ntap + 1) // 16) * 16
    toeplitz = pltpu.roll(
        jnp.broadcast_to(row, (starts, samples)), 0, 1, stride=1, stride_axis=0
    )
    residual = syn[...] - obs[...]
    r_high = residual.astype(jnp.bfloat16)
    r_low = (residual - r_high.astype(jnp.float32)).astype(jnp.bfloat16)
    t_high = toeplitz.astype(jnp.bfloat16)
    t_low = (toeplitz - t_high.astype(jnp.float32)).astype(jnp.bfloat16)
    all_starts = sum(
        lax.dot_general(a, b, NT_DIMS, preferred_element_type=jnp.float32)
        for a, b in ((t_high, r_low), (t_low, r_high), (t_high, r_high))
    )
    start = iota((starts, count), 0)
    offset = off[...]
    filtered = [
        jnp.sum(jnp.where(start == offset + step, all_starts, 0.0), axis=0, keepdims=True)
        for step in range(STEPS)
    ]
    both = jnp.concatenate(filtered + [jnp.zeros((8 - STEPS, count), jnp.float32)], axis=0)
    before = lines[0:1, :]
    after = lines[1:2, :]
    sources = jnp.zeros((8, count), jnp.float32)
    for reach in range(-SW, SW + 1):
        term = line_taps[0:1, reach + SW : reach + SW + 1] * (
            pltpu.roll(both, (-reach) % count, 1) if reach else both
        )
        if reach < 0:
            keep = (before >= -reach) & (place >= -reach)
        elif reach > 0:
            keep = (after >= reach) & (place < count - reach)
        else:
            keep = before >= 0
        sources = sources + jnp.where(keep, term, 0.0)
    cell = cells[...]
    high = (cell >> 8).astype(jnp.float32)
    low = (cell & 255).astype(jnp.float32)
    pieces = parts_of(sources[0:1], 3) + parts_of(sources[1:2], 3) + [high, low]
    spread = jnp.concatenate([pick16(owned, piece) for piece in pieces], axis=0)
    out = lax.dot_general(spread, slot, NT_DIMS, preferred_element_type=jnp.float32)
    part = [out[k * devices : (k + 1) * devices] for k in range(8)]
    value0 = part[0] + part[1] + part[2]
    value1 = part[3] + part[4] + part[5]
    where = 256.0 * part[6] + part[7]
    none = jnp.zeros((1, LANES), jnp.float32)

    def to_upper(rows):
        return pltpu.roll(jnp.concatenate([none, rows[:-1]], axis=0), LANES // 2, 1)

    def to_lower(rows):
        return pltpu.roll(jnp.concatenate([rows[1:], none], axis=0), LANES // 2, 1)

    def put(k, rows):
        for to, at in enumerate(place_of):
            send[at, k : k + 1, :] = rows[to : to + 1]

    put(0, value0 + to_upper(value0))
    put(1, where + to_upper(where))
    put(2, value1 + to_lower(value0))
    put(3, to_lower(where))
    count_ = jnp.where(place < SW, before, after).astype(jnp.float32)
    edge_rows = (
        parts_of(both[0:1], 3)
        + parts_of(both[1:2], 3)
        + [owner.astype(jnp.float32), high, low, count_]
    )
    edge_rows = jnp.concatenate(
        edge_rows + [jnp.zeros((16 - len(edge_rows), count), jnp.float32)], axis=0
    ).astype(jnp.bfloat16)
    edge = lax.dot_general(edge_rows, chosen, NT_DIMS, preferred_element_type=jnp.float32)
    edge_cell = edge[6:7] * float(block) + 256.0 * edge[7:8] + edge[8:9]
    shape = (devices, LANES)
    put(4, jnp.broadcast_to(edge[0:1] + edge[1:2] + edge[2:3], shape))
    put(5, jnp.broadcast_to(edge[3:4] + edge[4:5] + edge[5:6], shape))
    put(6, jnp.broadcast_to(edge_cell, shape))
    put(7, jnp.broadcast_to(edge[9:10], shape))
    sent = pltpu.make_async_copy(send, send_far, sems.at[0])
    sent.start()
    half_block(to_pair, (old.shape[0] - REACH) * (1 - me % 2), wide, vel, old)
    sent.wait()


def inner_kernel(
    old_far,
    now_far,
    vel_far,
    fwd_far,
    line_taps_far,
    partial,
    now,
    vel,
    weight0,
    weight1,
    line_taps,
    wide,
    old,
    fwd,
    sems,
):
    size_x, size_y, lanes = old.shape
    inside = slice(PAD, PAD + size_y)
    copies = started(
        sems,
        (now_far, wide.at[REACH : REACH + size_x, inside, :]),
        (vel_far, vel),
        (old_far, old),
        (fwd_far, fwd),
        (line_taps_far, line_taps),
    )
    edge = jnp.zeros((wide.shape[0], PAD, lanes), jnp.float32)
    wide[:, 0:PAD, :] = edge
    wide[:, PAD + size_y :, :] = edge
    blank = jnp.zeros((REACH, size_y, lanes), jnp.float32)
    wide[0:REACH, inside, :] = blank
    wide[REACH + size_x :, inside, :] = blank
    for copy in copies:
        copy.wait()

    for x in range(size_x):
        speed = vel[x]
        now[x] = wide[REACH + x, inside, :]
        partial[x] = (
            2.0 * now[x]
            - old[x]
            + squared(speed) * laplacian_plane(wide, x + REACH, size_y)
        )
        weight = 2.0 / (speed * speed * speed)
        f1 = fwd[1, x]
        f2 = fwd[2, x]
        weight0[x] = weight * (fwd[0, x] - 2.0 * f1 + f2)
        weight1[x] = weight * (f1 - 2.0 * f2 + fwd[3, x])


def across(field, x, low, high):
    total = None
    for k in range(1, 5):
        for at in (x - k, x + k):
            if low <= at < high:
                term = COEF[k] * field[at - low]
                total = term if total is None else total + term
    return total


def first_kernel(
    from_pair, from_next, partial, now, vel, free, scale
):
    odd = lax.axis_index("sub") % 2
    size_x = now.shape[0]
    from_next = Planes(from_next, now.shape[1])
    top = REACH + size_x

    def border(source, first_out, low):
        for i in range(REACH):
            factor = squared(source[2 * REACH + i])
            scale[first_out + i] = factor
            free[first_out + i] = source[REACH + i] + factor * across(now, low + i, 0, size_x)
        planes = range(REACH) if low < 0 else range(size_x - REACH, size_x)
        for x in planes:
            factor = squared(vel[x])
            scale[REACH + x] = factor
            free[REACH + x] = partial[x] + factor * across(source, x, low, low + REACH)

    @pl.when(odd == 0)
    def _():
        border(from_next, 0, -REACH)
        border(from_pair, top, size_x)

    @pl.when(odd == 1)
    def _():
        border(from_pair, 0, -REACH)
        border(from_next, top, size_x)


def second_kernel(
    devices,
    place_of,
    cap,
    got,
    free,
    scale,
    now,
    weight0,
    weight1,
    line_taps,
    prior_far,
    last_far,
    gradient_far,
    last,
    gradient,
    field,
    source1,
    out_sems,
):
    me = lax.axis_index("sub")
    size_x, size_y, lanes = now.shape
    rows = size_x * size_y
    halo = REACH * size_y
    block = rows * lanes
    pack = LANES // cap
    lane8 = iota((8, LANES), 1)
    shift = lanes.bit_length() - 1

    def hot_rows(cell, move, index):
        return hot16(index, (cell >> shift) + move)

    def spread(cell, values):
        at = same16(zs, cell & (lanes - 1))
        stack = []
        for value in values:
            for part in parts_of(value, 2):
                stack.append(pick16(at, part))
        return jnp.concatenate(stack, axis=0)

    def inject(a, b):
        return lax.dot_general(
            jnp.concatenate(a, axis=1),
            jnp.concatenate(b, axis=1),
            NT_DIMS,
            preferred_element_type=jnp.float32,
        )

    zs = index16(LANES, LANES)
    row_index = index16(rows, LANES)
    halo_index = index16(halo, LANES)

    own_a, own_b, low_a, low_b, high_a, high_b = [], [], [], [], [], []
    mine, other = [], []
    for g in range(devices // pack):
        tiles = [got[place_of[g * pack + q]] for q in range(pack)]
        one, two = tiles[0], tiles[pack // 2]
        for q in range(1, pack):
            later = lane8 >= q * cap
            one = jnp.where(later, tiles[q], one)
            two = jnp.where(later, tiles[(q + pack // 2) % pack], two)
        mine.append(one)
        other.append(two)
    for one in mine:
        cell = one[1:2].astype(jnp.int32)
        own_a.append(hot_rows(cell, 0, row_index))
        own_b.append(spread(cell, [one[0:1], one[2:3]]))
    for two in other:
        cell = two[1:2].astype(jnp.int32)
        low_a.append(hot_rows(cell, halo - rows, halo_index))
        low_b.append(spread(cell, [two[0:1]]))
    for two in other:
        cell = two[3:4].astype(jnp.int32)
        high_a.append(hot_rows(cell, 0, halo_index))
        high_b.append(spread(cell, [two[2:3]]))

    group = LANES // EDGE
    edge_parts = []
    for g in range(-(-devices // group)):
        total = got[place_of[g * group]]
        for i in range(g * group + 1, min(devices, (g + 1) * group)):
            total = total + got[place_of[i]]
        edge_parts.append(total)
    edge = jnp.concatenate(edge_parts, axis=1)
    width = edge.shape[1]
    spot = iota((8, width), 1)
    e = spot % EDGE
    count = edge[7:8]
    missing = jnp.zeros((8, width), jnp.float32)
    for reach in range(-SW, SW + 1):
        if reach == 0:
            continue
        if reach < 0:
            crosses = (e < -reach) & (spot >= -reach)
        else:
            crosses = (e >= EDGE - reach) & (spot < width - reach)
        keep = crosses & (count >= float(abs(reach)))
        missing = missing + jnp.where(
            keep,
            line_taps[0:1, reach + SW : reach + SW + 1] * pltpu.roll(edge, (-reach) % width, 1),
            0.0,
        )
    edge_cell = edge[6:7].astype(jnp.int32) - me * block
    edge_row = jnp.clip(edge_cell >> shift, -2 * rows, 2 * rows)
    for g in range(width // LANES):
        at = slice(g * LANES, (g + 1) * LANES)
        b = spread(edge_cell[:, at], [missing[4:5, at], missing[5:6, at]])
        own_a.append(hot16(row_index, edge_row[:, at]))
        own_b.append(b)
        low_a.append(hot16(halo_index, edge_row[:, at] + halo))
        low_b.append(b[: 2 * LANES])
        high_a.append(hot16(halo_index, edge_row[:, at] - rows))
        high_b.append(b[: 2 * LANES])

    zeros = jnp.zeros((field.shape[0], PAD, lanes), jnp.float32)
    field[:, 0:PAD, :] = zeros
    field[:, PAD + size_y :, :] = zeros
    inside = slice(PAD, PAD + size_y)
    top = REACH + size_x

    out = inject(own_a, own_b)
    low_out = inject(low_a, low_b)
    high_out = inject(high_a, high_b)
    first = (out[:, 0:lanes] + out[:, lanes : 2 * lanes]).reshape(size_x, size_y, lanes)
    source1[...] = (out[:, 2 * lanes : 3 * lanes] + out[:, 3 * lanes :]).reshape(
        size_x, size_y, lanes
    )
    field[REACH:top, inside, :] = free[REACH:top] + scale[REACH:top] * first
    done = [
        pltpu.make_async_copy(field.at[REACH:top, inside, :], prior_far, out_sems.at[0])
    ]
    done[0].start()
    first = (low_out[:, 0:lanes] + low_out[:, lanes:]).reshape(REACH, size_y, lanes)
    field[0:REACH, inside, :] = free[0:REACH] + scale[0:REACH] * first
    first = (high_out[:, 0:lanes] + high_out[:, lanes:]).reshape(REACH, size_y, lanes)
    field[top:, inside, :] = free[top:] + scale[top:] * first

    half = size_x // 2
    for part in range(2):
        planes = slice(part * half, (part + 1) * half)

        for x in range(part * half, (part + 1) * half):
            at = x + REACH
            fresh = field[at, inside, :]
            following = (
                2.0 * fresh
                - now[x]
                + scale[at] * (laplacian_plane(field, at, size_y) + source1[x])
            )
            last[x] = following
            gradient[x] = weight0[x] * fresh + weight1[x] * following

        done += started(
            out_sems.at[pl.ds(1 + 2 * part, 2)],
            (last.at[planes], last_far.at[planes]),
            (gradient.at[planes], gradient_far.at[planes]),
        )
    for copy in done:
        copy.wait()


def body(
    synthetic,
    observed,
    offsets,
    lines,
    owners,
    cells,
    taps,
    line_taps,
    velocity,
    adjoint_old,
    adjoint_now,
    forward,
):
    count = synthetic.shape[0]
    size_x, size_y, lanes = velocity.shape
    devices = lax.axis_size("sub")
    cap = max(2, 2 * count // devices)
    f32 = jnp.float32

    order = list(range(devices))[::-1]
    place_of = [order.index(i) for i in range(devices)]
    pair = [(i, i ^ 1) for i in range(devices)]
    following = [(i, i + 1) for i in range(1, devices - 1, 2)]
    following = following + [(b, a) for a, b in following]

    plane = (size_y, lanes)
    outer = size_x + 2 * REACH
    inner = pltpu.VMEM((size_x,) + plane, f32)
    padded = pltpu.VMEM((outer, size_y + 2 * PAD, lanes), f32)
    halo = pltpu.VMEM((3 * REACH,) + plane, f32)
    wider = pltpu.VMEM((outer,) + plane, f32)
    inner_far = pltpu.HBM((size_x,) + plane, f32)
    wider_far = pltpu.HBM((outer,) + plane, f32)
    dma = pltpu.SemaphoreType.DMA

    row = (1, count)
    sources = (
        adjoint_now,
        velocity,
        adjoint_old,
        owners.reshape(row),
        cells.reshape(row),
        taps.reshape(1, -1),
        offsets.reshape(row),
        lines,
        line_taps.reshape(1, -1),
        synthetic,
        observed,
    )
    fetched = (padded,) + tuple(pltpu.VMEM(a.shape, a.dtype) for a in sources[1:])
    to_next, *fetched = pl.pallas_call(
        next_kernel,
        out_shape=(pltpu.VMEM((3 * REACH * size_y + 8, lanes), f32),) + fetched,
        in_specs=[FAR] * len(sources),
        out_specs=(VMEM,) * (1 + len(sources)),
        scratch_shapes=[dma((len(sources),))],
        compiler_params=PARAMS,
        name="next",
    )(*far(*sources))
    send, to_pair = pl.pallas_call(
        functools.partial(send_kernel, devices, place_of, cap, velocity.size),
        out_shape=(pltpu.HBM((devices, 8, LANES), f32), halo),
        in_specs=[VMEM] * len(fetched),
        out_specs=(FAR, VMEM),
        scratch_shapes=[pltpu.VMEM((devices, 8, LANES), f32), dma((1,))],
        compiler_params=PARAMS,
        name="send",
    )(*(near(a) for a in fetched))
    from_next = lax.ppermute(to_next, "sub", following)
    from_pair = lax.ppermute(to_pair, "sub", pair)
    got = lax.all_to_all(
        send, "sub", split_axis=0, concat_axis=0, axis_index_groups=[order], tiled=True
    )

    partial, now, vel, weight0, weight1, line_row = pl.pallas_call(
        inner_kernel,
        out_shape=(inner,) * 5 + (pltpu.VMEM((1, line_taps.shape[0]), f32),),
        in_specs=[FAR] * 5,
        out_specs=(VMEM,) * 6,
        scratch_shapes=[padded, inner, pltpu.VMEM(forward.shape, f32), dma((5,))],
        compiler_params=PARAMS,
        name="inner",
    )(*far(adjoint_old, adjoint_now, velocity, forward, line_taps.reshape(1, -1)))
    free, scale = pl.pallas_call(
        first_kernel,
        out_shape=(wider,) * 2,
        in_specs=[VMEM] * 5,
        out_specs=(VMEM,) * 2,
        compiler_params=PARAMS,
        name="first",
    )(near(from_pair), near(from_next), near(partial), near(now), near(vel))

    field = jax.ShapeDtypeStruct((size_x,) + plane, f32)
    return pl.pallas_call(
        functools.partial(second_kernel, devices, place_of, cap),
        out_shape=(field, field, field),
        in_specs=[VMEM] * 7,
        out_specs=(FAR,) * 3,
        scratch_shapes=[
            inner,
            inner,
            pltpu.VMEM((outer, size_y + 2 * PAD, lanes), f32),
            inner,
            dma((5,)),
        ],
        compiler_params=PARAMS,
        name="second",
    )(
        near(got),
        near(free),
        near(scale),
        near(now),
        near(weight0),
        near(weight1),
        near(line_row),
    )


def solution(mesh):
    return jax.shard_map(
        body,
        mesh=mesh,
        in_specs=(
            P(("shot", "sub"), None),
            P(("shot", "sub"), None),
            P(("shot", "sub")),
            P(None, ("shot", "sub")),
            P(("shot", "sub"), None),
            P(("shot", "sub")),
            P(),
            P(),
            P("sub", None, None),
            P(("shot", "sub"), None, None),
            P(("shot", "sub"), None, None),
            P(None, ("shot", "sub"), None, None),
        ),
        out_specs=(
            P(("shot", "sub"), None, None),
            P(("shot", "sub"), None, None),
            P(("shot", "sub"), None, None),
        ),
        check_vma=False,
    )
```

```python
import functools

import jax
import jax.numpy as jnp
from jax import lax
from jax.experimental import pallas as pl
from jax.experimental.pallas import tpu as pltpu
from jax.sharding import PartitionSpec as P

SW = 4
STEPS = 2
REACH = 4
LANES = 128
EDGE = 2 * SW

COEF = (-205.0 / 72.0, 8.0 / 5.0, -1.0 / 5.0, 8.0 / 315.0, -1.0 / 560.0)
DT_OVER_H = 0.18

VMEM = pl.BlockSpec(memory_space=pltpu.VMEM)
FAR = pl.BlockSpec(memory_space=pltpu.HBM)
PARAMS = pltpu.CompilerParams(vmem_limit_bytes=16 * 2**20)
NT_DIMS = (((1,), (1,)), ((), ()))


def near(array):
    return pltpu.with_memory_space_constraint(array, pltpu.VMEM)


def far(*arrays):
    return [pltpu.with_memory_space_constraint(array, pltpu.HBM) for array in arrays]


def started(sems, *pairs):
    copies = [
        pltpu.make_async_copy(source, target, sems.at[i])
        for i, (source, target) in enumerate(pairs)
    ]
    for copy in copies:
        copy.start()
    return copies


def parts_of(value, count):
    parts = []
    for _ in range(count):
        part = value.astype(jnp.bfloat16).astype(jnp.float32)
        parts.append(part)
        value = value - part
    return parts


def iota(shape, axis):
    return lax.broadcasted_iota(jnp.int32, shape, axis)


PACKED = 16


def across16(row):
    return jnp.broadcast_to(row, (PACKED, row.shape[1])).astype(jnp.int16)[None]


def index16(count, width):
    rows = iota((count, width), 0).astype(jnp.int16)
    return rows.reshape(count // PACKED, PACKED, width)


def same16(index, row):
    return index == across16(row)


def pick16(mask, row):
    width = row.shape[1]
    wide = jnp.broadcast_to(row, (PACKED, width)).astype(jnp.bfloat16)
    picked = jnp.where(mask, wide[None], jnp.zeros((), jnp.bfloat16))
    return picked.reshape(-1, width)


def hot16(index, row):
    return pick16(same16(index, row), jnp.ones(row.shape, jnp.float32))


PAD = 8


class Planes:
    def __init__(self, rows, height):
        self.rows, self.height = rows, height

    def __getitem__(self, i):
        return self.rows[i * self.height : (i + 1) * self.height, :]

    def __setitem__(self, i, value):
        self.rows[i * self.height : (i + 1) * self.height, :] = value


def laplacian_plane(field, x, size_y):
    centre = field[x, PAD : PAD + size_y, :]
    lanes = centre.shape[1]
    lane = iota(centre.shape, 1)
    total = 3.0 * COEF[0] * centre
    for k in range(1, 5):
        near = field[x + k, PAD : PAD + size_y, :] + field[x - k, PAD : PAD + size_y, :]
        near = near + field[x, PAD + k : PAD + k + size_y, :]
        near = near + field[x, PAD - k : PAD - k + size_y, :]
        near = near + jnp.where(lane < lanes - k, pltpu.roll(centre, lanes - k, 1), 0.0)
        near = near + jnp.where(lane >= k, pltpu.roll(centre, k, 1), 0.0)
        total = total + COEF[k] * near
    return total


def squared(speed):
    factor = DT_OVER_H * speed
    return factor * factor


def half_block(target, start, wide, vel, old):
    size_y = old.shape[1]
    inside = slice(PAD, PAD + size_y)
    for i in range(REACH):
        x = start + i
        own_now = wide[REACH + x, inside, :]
        speed = vel[x]
        target[i] = own_now
        target[REACH + i] = (
            2.0 * own_now
            - old[x]
            + squared(speed) * laplacian_plane(wide, x + REACH, size_y)
        )
        target[2 * REACH + i] = speed


def next_kernel(
    now_far,
    vel_far,
    old_far,
    own_far,
    cells_far,
    taps_far,
    off_far,
    lines_far,
    line_taps_far,
    syn_far,
    obs_far,
    to_next,
    wide,
    vel,
    old,
    own,
    cells,
    taps,
    off,
    lines,
    line_taps,
    syn,
    obs,
    sems,
):
    size_x, size_y, lanes = old.shape
    inside = slice(PAD, PAD + size_y)
    copies = started(
        sems,
        (now_far, wide.at[REACH : REACH + size_x, inside, :]),
        (vel_far, vel),
        (old_far, old),
        (own_far, own),
        (cells_far, cells),
        (taps_far, taps),
        (off_far, off),
        (lines_far, lines),
        (line_taps_far, line_taps),
        (syn_far, syn),
        (obs_far, obs),
    )
    edge = jnp.zeros((wide.shape[0], PAD, lanes), jnp.float32)
    wide[:, 0:PAD, :] = edge
    wide[:, PAD + size_y :, :] = edge
    blank = jnp.zeros((REACH, size_y, lanes), jnp.float32)
    wide[0:REACH, inside, :] = blank
    wide[REACH + size_x :, inside, :] = blank
    for copy in copies[:3]:
        copy.wait()
    odd = lax.axis_index("sub") % 2
    used = 3 * REACH * size_y
    to_next[used:, :] = jnp.zeros((to_next.shape[0] - used, lanes), jnp.float32)
    half_block(Planes(to_next, size_y), (size_x - REACH) * odd, wide, vel, old)
    for copy in copies[3:]:
        copy.wait()


def send_kernel(
    devices,
    place_of,
    cap,
    block,
    wide,
    vel,
    old,
    own,
    cells,
    taps,
    off,
    lines,
    line_taps,
    syn,
    obs,
    send_far,
    to_pair,
    send,
    sems,
):
    me = lax.axis_index("sub")
    count, samples = syn.shape
    ntap = taps.shape[1]
    pack = LANES // cap
    group = LANES // EDGE
    place = iota((1, count), 1)
    owner = own[...]
    owned = same16(index16(devices, count), owner)
    one_hot = pick16(owned, jnp.ones((1, count), jnp.float32))
    chunks = [one_hot[:, at : at + LANES] for at in range(0, count, LANES)]
    ahead = index16(LANES, LANES) < across16(iota((1, LANES), 1))
    ranks = jnp.dot(
        jnp.concatenate(chunks, axis=0),
        pick16(ahead, jnp.ones((1, LANES), jnp.float32)),
        preferred_element_type=jnp.float32,
    )
    base = jnp.zeros((devices, 1), jnp.float32)
    rank = []
    for i, chunk in enumerate(chunks):
        chunk = chunk.astype(jnp.float32)
        rank.append(
            jnp.sum(
                chunk * (ranks[i * devices : (i + 1) * devices] + base), axis=0, keepdims=True
            )
        )
        base = base + jnp.sum(chunk, axis=1, keepdims=True)
    rank = jnp.concatenate(rank, axis=1).astype(jnp.int32)
    lane = index16(LANES, count)
    slot = hot16(lane, rank + (me % pack) * cap)
    edge_lane = jnp.where(
        place < SW, place, jnp.where(place >= count - SW, place - count + EDGE, -LANES)
    )
    chosen = hot16(lane, edge_lane + (me % group) * EDGE)

    row = jnp.concatenate([taps[...], jnp.zeros((1, samples - ntap), jnp.float32)], axis=1)
    starts = -(-(samples - ntap + 1) // 16) * 16
    toeplitz = pltpu.roll(
        jnp.broadcast_to(row, (starts, samples)), 0, 1, stride=1, stride_axis=0
    )
    residual = syn[...] - obs[...]
    r_high = residual.astype(jnp.bfloat16)
    r_low = (residual - r_high.astype(jnp.float32)).astype(jnp.bfloat16)
    t_high = toeplitz.astype(jnp.bfloat16)
    t_low = (toeplitz - t_high.astype(jnp.float32)).astype(jnp.bfloat16)
    all_starts = sum(
        lax.dot_general(a, b, NT_DIMS, preferred_element_type=jnp.float32)
        for a, b in ((t_high, r_low), (t_low, r_high), (t_high, r_high))
    )
    start = iota((starts, count), 0)
    offset = off[...]
    filtered = [
        jnp.sum(jnp.where(start == offset + step, all_starts, 0.0), axis=0, keepdims=True)
        for step in range(STEPS)
    ]
    both = jnp.concatenate(filtered + [jnp.zeros((8 - STEPS, count), jnp.float32)], axis=0)
    before = lines[0:1, :]
    after = lines[1:2, :]
    sources = jnp.zeros((8, count), jnp.float32)
    for reach in range(-SW, SW + 1):
        term = line_taps[0:1, reach + SW : reach + SW + 1] * (
            pltpu.roll(both, (-reach) % count, 1) if reach else both
        )
        if reach < 0:
            keep = (before >= -reach) & (place >= -reach)
        elif reach > 0:
            keep = (after >= reach) & (place < count - reach)
        else:
            keep = before >= 0
        sources = sources + jnp.where(keep, term, 0.0)
    cell = cells[...]
    high = (cell >> 8).astype(jnp.float32)
    low = (cell & 255).astype(jnp.float32)
    pieces = parts_of(sources[0:1], 3) + parts_of(sources[1:2], 3) + [high, low]
    spread = jnp.concatenate([pick16(owned, piece) for piece in pieces], axis=0)
    out = lax.dot_general(spread, slot, NT_DIMS, preferred_element_type=jnp.float32)
    part = [out[k * devices : (k + 1) * devices] for k in range(8)]
    value0 = part[0] + part[1] + part[2]
    value1 = part[3] + part[4] + part[5]
    where = 256.0 * part[6] + part[7]
    none = jnp.zeros((1, LANES), jnp.float32)

    def to_upper(rows):
        return pltpu.roll(jnp.concatenate([none, rows[:-1]], axis=0), LANES // 2, 1)

    def to_lower(rows):
        return pltpu.roll(jnp.concatenate([rows[1:], none], axis=0), LANES // 2, 1)

    def put(k, rows):
        for to, at in enumerate(place_of):
            send[at, k : k + 1, :] = rows[to : to + 1]

    put(0, value0 + to_upper(value0))
    put(1, where + to_upper(where))
    put(2, value1 + to_lower(value0))
    put(3, to_lower(where))
    count_ = jnp.where(place < SW, before, after).astype(jnp.float32)
    edge_rows = (
        parts_of(both[0:1], 3)
        + parts_of(both[1:2], 3)
        + [owner.astype(jnp.float32), high, low, count_]
    )
    edge_rows = jnp.concatenate(
        edge_rows + [jnp.zeros((16 - len(edge_rows), count), jnp.float32)], axis=0
    ).astype(jnp.bfloat16)
    edge = lax.dot_general(edge_rows, chosen, NT_DIMS, preferred_element_type=jnp.float32)
    edge_cell = edge[6:7] * float(block) + 256.0 * edge[7:8] + edge[8:9]
    shape = (devices, LANES)
    put(4, jnp.broadcast_to(edge[0:1] + edge[1:2] + edge[2:3], shape))
    put(5, jnp.broadcast_to(edge[3:4] + edge[4:5] + edge[5:6], shape))
    put(6, jnp.broadcast_to(edge_cell, shape))
    put(7, jnp.broadcast_to(edge[9:10], shape))
    sent = pltpu.make_async_copy(send, send_far, sems.at[0])
    sent.start()
    half_block(to_pair, (old.shape[0] - REACH) * (1 - me % 2), wide, vel, old)
    sent.wait()


def inner_kernel(
    old_far,
    now_far,
    vel_far,
    fwd_far,
    line_taps_far,
    partial,
    now,
    vel,
    weight0,
    weight1,
    line_taps,
    wide,
    old,
    fwd,
    sems,
):
    size_x, size_y, lanes = old.shape
    inside = slice(PAD, PAD + size_y)
    copies = started(
        sems,
        (now_far, wide.at[REACH : REACH + size_x, inside, :]),
        (vel_far, vel),
        (old_far, old),
        (fwd_far, fwd),
        (line_taps_far, line_taps),
    )
    edge = jnp.zeros((wide.shape[0], PAD, lanes), jnp.float32)
    wide[:, 0:PAD, :] = edge
    wide[:, PAD + size_y :, :] = edge
    blank = jnp.zeros((REACH, size_y, lanes), jnp.float32)
    wide[0:REACH, inside, :] = blank
    wide[REACH + size_x :, inside, :] = blank
    for copy in copies:
        copy.wait()

    for x in range(size_x):
        speed = vel[x]
        now[x] = wide[REACH + x, inside, :]
        partial[x] = (
            2.0 * now[x]
            - old[x]
            + squared(speed) * laplacian_plane(wide, x + REACH, size_y)
        )
        weight = 2.0 / (speed * speed * speed)
        f1 = fwd[1, x]
        f2 = fwd[2, x]
        weight0[x] = weight * (fwd[0, x] - 2.0 * f1 + f2)
        weight1[x] = weight * (f1 - 2.0 * f2 + fwd[3, x])


def across(field, x, low, high):
    total = None
    for k in range(1, 5):
        for at in (x - k, x + k):
            if low <= at < high:
                term = COEF[k] * field[at - low]
                total = term if total is None else total + term
    return total


def first_kernel(
    from_pair, from_next, partial, now, vel, free, scale
):
    odd = lax.axis_index("sub") % 2
    size_x = now.shape[0]
    from_next = Planes(from_next, now.shape[1])
    top = REACH + size_x

    def border(source, first_out, low):
        for i in range(REACH):
            factor = squared(source[2 * REACH + i])
            scale[first_out + i] = factor
            free[first_out + i] = source[REACH + i] + factor * across(now, low + i, 0, size_x)
        planes = range(REACH) if low < 0 else range(size_x - REACH, size_x)
        for x in planes:
            factor = squared(vel[x])
            scale[REACH + x] = factor
            free[REACH + x] = partial[x] + factor * across(source, x, low, low + REACH)

    @pl.when(odd == 0)
    def _():
        border(from_next, 0, -REACH)
        border(from_pair, top, size_x)

    @pl.when(odd == 1)
    def _():
        border(from_pair, 0, -REACH)
        border(from_next, top, size_x)


def second_kernel(
    devices,
    place_of,
    cap,
    got,
    free,
    scale,
    now,
    weight0,
    weight1,
    line_taps,
    prior_far,
    last_far,
    gradient_far,
    last,
    gradient,
    field,
    source1,
    out_sems,
):
    me = lax.axis_index("sub")
    size_x, size_y, lanes = now.shape
    rows = size_x * size_y
    halo = REACH * size_y
    block = rows * lanes
    pack = LANES // cap
    lane8 = iota((8, LANES), 1)
    shift = lanes.bit_length() - 1

    def hot_rows(cell, move, index):
        return hot16(index, (cell >> shift) + move)

    def spread(cell, values):
        at = same16(zs, cell & (lanes - 1))
        stack = []
        for value in values:
            for part in parts_of(value, 2):
                stack.append(pick16(at, part))
        return jnp.concatenate(stack, axis=0)

    def inject(a, b):
        return lax.dot_general(
            jnp.concatenate(a, axis=1),
            jnp.concatenate(b, axis=1),
            NT_DIMS,
            preferred_element_type=jnp.float32,
        )

    zs = index16(LANES, LANES)
    row_index = index16(rows, LANES)
    halo_index = index16(halo, LANES)

    own_a, own_b, low_a, low_b, high_a, high_b = [], [], [], [], [], []
    mine, other = [], []
    for g in range(devices // pack):
        tiles = [got[place_of[g * pack + q]] for q in range(pack)]
        one, two = tiles[0], tiles[pack // 2]
        for q in range(1, pack):
            later = lane8 >= q * cap
            one = jnp.where(later, tiles[q], one)
            two = jnp.where(later, tiles[(q + pack // 2) % pack], two)
        mine.append(one)
        other.append(two)
    for one in mine:
        cell = one[1:2].astype(jnp.int32)
        own_a.append(hot_rows(cell, 0, row_index))
        own_b.append(spread(cell, [one[0:1], one[2:3]]))
    for two in other:
        cell = two[1:2].astype(jnp.int32)
        low_a.append(hot_rows(cell, halo - rows, halo_index))
        low_b.append(spread(cell, [two[0:1]]))
    for two in other:
        cell = two[3:4].astype(jnp.int32)
        high_a.append(hot_rows(cell, 0, halo_index))
        high_b.append(spread(cell, [two[2:3]]))

    group = LANES // EDGE
    edge_parts = []
    for g in range(-(-devices // group)):
        total = got[place_of[g * group]]
        for i in range(g * group + 1, min(devices, (g + 1) * group)):
            total = total + got[place_of[i]]
        edge_parts.append(total)
    edge = jnp.concatenate(edge_parts, axis=1)
    width = edge.shape[1]
    spot = iota((8, width), 1)
    e = spot % EDGE
    count = edge[7:8]
    missing = jnp.zeros((8, width), jnp.float32)
    for reach in range(-SW, SW + 1):
        if reach == 0:
            continue
        if reach < 0:
            crosses = (e < -reach) & (spot >= -reach)
        else:
            crosses = (e >= EDGE - reach) & (spot < width - reach)
        keep = crosses & (count >= float(abs(reach)))
        missing = missing + jnp.where(
            keep,
            line_taps[0:1, reach + SW : reach + SW + 1] * pltpu.roll(edge, (-reach) % width, 1),
            0.0,
        )
    edge_cell = edge[6:7].astype(jnp.int32) - me * block
    edge_row = jnp.clip(edge_cell >> shift, -2 * rows, 2 * rows)
    for g in range(width // LANES):
        at = slice(g * LANES, (g + 1) * LANES)
        b = spread(edge_cell[:, at], [missing[4:5, at], missing[5:6, at]])
        own_a.append(hot16(row_index, edge_row[:, at]))
        own_b.append(b)
        low_a.append(hot16(halo_index, edge_row[:, at] + halo))
        low_b.append(b[: 2 * LANES])
        high_a.append(hot16(halo_index, edge_row[:, at] - rows))
        high_b.append(b[: 2 * LANES])

    zeros = jnp.zeros((field.shape[0], PAD, lanes), jnp.float32)
    field[:, 0:PAD, :] = zeros
    field[:, PAD + size_y :, :] = zeros
    inside = slice(PAD, PAD + size_y)
    top = REACH + size_x

    out = inject(own_a, own_b)
    low_out = inject(low_a, low_b)
    high_out = inject(high_a, high_b)
    first = (out[:, 0:lanes] + out[:, lanes : 2 * lanes]).reshape(size_x, size_y, lanes)
    source1[...] = (out[:, 2 * lanes : 3 * lanes] + out[:, 3 * lanes :]).reshape(
        size_x, size_y, lanes
    )
    field[REACH:top, inside, :] = free[REACH:top] + scale[REACH:top] * first
    done = [
        pltpu.make_async_copy(field.at[REACH:top, inside, :], prior_far, out_sems.at[0])
    ]
    done[0].start()
    first = (low_out[:, 0:lanes] + low_out[:, lanes:]).reshape(REACH, size_y, lanes)
    field[0:REACH, inside, :] = free[0:REACH] + scale[0:REACH] * first
    first = (high_out[:, 0:lanes] + high_out[:, lanes:]).reshape(REACH, size_y, lanes)
    field[top:, inside, :] = free[top:] + scale[top:] * first

    cuts = (0, size_x // 2, size_x - 1, size_x)
    for part in range(3):
        planes = slice(cuts[part], cuts[part + 1])

        for x in range(cuts[part], cuts[part + 1]):
            at = x + REACH
            fresh = field[at, inside, :]
            following = (
                2.0 * fresh
                - now[x]
                + scale[at] * (laplacian_plane(field, at, size_y) + source1[x])
            )
            last[x] = following
            gradient[x] = weight0[x] * fresh + weight1[x] * following

        done += started(
            out_sems.at[pl.ds(1 + 2 * part, 2)],
            (last.at[planes], last_far.at[planes]),
            (gradient.at[planes], gradient_far.at[planes]),
        )
    for copy in done:
        copy.wait()


def body(
    synthetic,
    observed,
    offsets,
    lines,
    owners,
    cells,
    taps,
    line_taps,
    velocity,
    adjoint_old,
    adjoint_now,
    forward,
):
    count = synthetic.shape[0]
    size_x, size_y, lanes = velocity.shape
    devices = lax.axis_size("sub")
    cap = max(2, 2 * count // devices)
    f32 = jnp.float32

    order = list(range(1, devices, 2))[::-1] + list(range(0, devices, 2))[::-1]
    place_of = [order.index(i) for i in range(devices)]
    pair = [(i, i ^ 1) for i in range(devices)]
    following = [(i, i + 1) for i in range(1, devices - 1, 2)]
    following = following + [(b, a) for a, b in following]

    plane = (size_y, lanes)
    outer = size_x + 2 * REACH
    inner = pltpu.VMEM((size_x,) + plane, f32)
    padded = pltpu.VMEM((outer, size_y + 2 * PAD, lanes), f32)
    halo = pltpu.VMEM((3 * REACH,) + plane, f32)
    wider = pltpu.VMEM((outer,) + plane, f32)
    inner_far = pltpu.HBM((size_x,) + plane, f32)
    wider_far = pltpu.HBM((outer,) + plane, f32)
    dma = pltpu.SemaphoreType.DMA

    row = (1, count)
    sources = (
        adjoint_now,
        velocity,
        adjoint_old,
        owners.reshape(row),
        cells.reshape(row),
        taps.reshape(1, -1),
        offsets.reshape(row),
        lines,
        line_taps.reshape(1, -1),
        synthetic,
        observed,
    )
    fetched = (padded,) + tuple(pltpu.VMEM(a.shape, a.dtype) for a in sources[1:])
    to_next, *fetched = pl.pallas_call(
        next_kernel,
        out_shape=(pltpu.VMEM((3 * REACH * size_y + 8, lanes), f32),) + fetched,
        in_specs=[FAR] * len(sources),
        out_specs=(VMEM,) * (1 + len(sources)),
        scratch_shapes=[dma((len(sources),))],
        compiler_params=PARAMS,
        name="next",
    )(*far(*sources))
    send, to_pair = pl.pallas_call(
        functools.partial(send_kernel, devices, place_of, cap, velocity.size),
        out_shape=(pltpu.HBM((devices, 8, LANES), f32), halo),
        in_specs=[VMEM] * len(fetched),
        out_specs=(FAR, VMEM),
        scratch_shapes=[pltpu.VMEM((devices, 8, LANES), f32), dma((1,))],
        compiler_params=PARAMS,
        name="send",
    )(*(near(a) for a in fetched))
    from_next = lax.ppermute(to_next, "sub", following)
    from_pair = lax.ppermute(to_pair, "sub", pair)
    got = lax.all_to_all(
        send, "sub", split_axis=0, concat_axis=0, axis_index_groups=[order], tiled=True
    )

    partial, now, vel, weight0, weight1, line_row = pl.pallas_call(
        inner_kernel,
        out_shape=(inner,) * 5 + (pltpu.VMEM((1, line_taps.shape[0]), f32),),
        in_specs=[FAR] * 5,
        out_specs=(VMEM,) * 6,
        scratch_shapes=[padded, inner, pltpu.VMEM(forward.shape, f32), dma((5,))],
        compiler_params=PARAMS,
        name="inner",
    )(*far(adjoint_old, adjoint_now, velocity, forward, line_taps.reshape(1, -1)))
    free, scale = pl.pallas_call(
        first_kernel,
        out_shape=(wider,) * 2,
        in_specs=[VMEM] * 5,
        out_specs=(VMEM,) * 2,
        compiler_params=PARAMS,
        name="first",
    )(near(from_pair), near(from_next), near(partial), near(now), near(vel))

    field = jax.ShapeDtypeStruct((size_x,) + plane, f32)
    return pl.pallas_call(
        functools.partial(second_kernel, devices, place_of, cap),
        out_shape=(field, field, field),
        in_specs=[VMEM] * 7,
        out_specs=(FAR,) * 3,
        scratch_shapes=[
            inner,
            inner,
            pltpu.VMEM((outer, size_y + 2 * PAD, lanes), f32),
            inner,
            dma((7,)),
        ],
        compiler_params=PARAMS,
        name="second",
    )(
        near(got),
        near(free),
        near(scale),
        near(now),
        near(weight0),
        near(weight1),
        near(line_row),
    )


def solution(mesh):
    return jax.shard_map(
        body,
        mesh=mesh,
        in_specs=(
            P(("shot", "sub"), None),
            P(("shot", "sub"), None),
            P(("shot", "sub")),
            P(None, ("shot", "sub")),
            P(("shot", "sub"), None),
            P(("shot", "sub")),
            P(),
            P(),
            P("sub", None, None),
            P(("shot", "sub"), None, None),
            P(("shot", "sub"), None, None),
            P(None, ("shot", "sub"), None, None),
        ),
        out_specs=(
            P(("shot", "sub"), None, None),
            P(("shot", "sub"), None, None),
            P(("shot", "sub"), None, None),
        ),
        check_vma=False,
    )
```

```python
import functools

import jax
import jax.numpy as jnp
from jax import lax
from jax.experimental import pallas as pl
from jax.experimental.pallas import tpu as pltpu
from jax.sharding import PartitionSpec as P

SW = 4
STEPS = 2
REACH = 4
LANES = 128
EDGE = 2 * SW

COEF = (-205.0 / 72.0, 8.0 / 5.0, -1.0 / 5.0, 8.0 / 315.0, -1.0 / 560.0)
DT_OVER_H = 0.18

VMEM = pl.BlockSpec(memory_space=pltpu.VMEM)
FAR = pl.BlockSpec(memory_space=pltpu.HBM)
PARAMS = pltpu.CompilerParams(vmem_limit_bytes=16 * 2**20)
NT_DIMS = (((1,), (1,)), ((), ()))


def near(array):
    return pltpu.with_memory_space_constraint(array, pltpu.VMEM)


def far(*arrays):
    return [pltpu.with_memory_space_constraint(array, pltpu.HBM) for array in arrays]


def started(sems, *pairs):
    copies = [
        pltpu.make_async_copy(source, target, sems.at[i])
        for i, (source, target) in enumerate(pairs)
    ]
    for copy in copies:
        copy.start()
    return copies


def parts_of(value, count):
    parts = []
    for _ in range(count):
        part = value.astype(jnp.bfloat16).astype(jnp.float32)
        parts.append(part)
        value = value - part
    return parts


def iota(shape, axis):
    return lax.broadcasted_iota(jnp.int32, shape, axis)


PACKED = 16


def across16(row):
    return jnp.broadcast_to(row, (PACKED, row.shape[1])).astype(jnp.int16)[None]


def index16(count, width):
    rows = iota((count, width), 0).astype(jnp.int16)
    return rows.reshape(count // PACKED, PACKED, width)


def same16(index, row):
    return index == across16(row)


def pick16(mask, row):
    width = row.shape[1]
    wide = jnp.broadcast_to(row, (PACKED, width)).astype(jnp.bfloat16)
    picked = jnp.where(mask, wide[None], jnp.zeros((), jnp.bfloat16))
    return picked.reshape(-1, width)


def hot16(index, row):
    return pick16(same16(index, row), jnp.ones(row.shape, jnp.float32))


PAD = 8


class Planes:
    def __init__(self, rows, height):
        self.rows, self.height = rows, height

    def __getitem__(self, i):
        return self.rows[i * self.height : (i + 1) * self.height, :]

    def __setitem__(self, i, value):
        self.rows[i * self.height : (i + 1) * self.height, :] = value


def laplacian_plane(field, x, size_y):
    centre = field[x, PAD : PAD + size_y, :]
    lanes = centre.shape[1]
    lane = iota(centre.shape, 1)
    total = 3.0 * COEF[0] * centre
    for k in range(1, 5):
        near = field[x + k, PAD : PAD + size_y, :] + field[x - k, PAD : PAD + size_y, :]
        near = near + field[x, PAD + k : PAD + k + size_y, :]
        near = near + field[x, PAD - k : PAD - k + size_y, :]
        near = near + jnp.where(lane < lanes - k, pltpu.roll(centre, lanes - k, 1), 0.0)
        near = near + jnp.where(lane >= k, pltpu.roll(centre, k, 1), 0.0)
        total = total + COEF[k] * near
    return total


def squared(speed):
    factor = DT_OVER_H * speed
    return factor * factor


def half_block(target, start, wide, vel, old):
    size_y = old.shape[1]
    inside = slice(PAD, PAD + size_y)
    for i in range(REACH):
        x = start + i
        own_now = wide[REACH + x, inside, :]
        speed = vel[x]
        target[i] = own_now
        target[REACH + i] = (
            2.0 * own_now
            - old[x]
            + squared(speed) * laplacian_plane(wide, x + REACH, size_y)
        )
        target[2 * REACH + i] = speed


def next_kernel(
    now_far,
    vel_far,
    old_far,
    own_far,
    cells_far,
    taps_far,
    off_far,
    lines_far,
    line_taps_far,
    syn_far,
    obs_far,
    to_next,
    wide,
    vel,
    old,
    own,
    cells,
    taps,
    off,
    lines,
    line_taps,
    syn,
    obs,
    sems,
):
    piece = syn.shape[0] // 2
    cuts = [pl.ds(i * piece, piece) for i in range(2)]
    size_x, size_y, lanes = old.shape
    inside = slice(PAD, PAD + size_y)
    copies = started(
        sems,
        (now_far, wide.at[REACH : REACH + size_x, inside, :]),
        (vel_far, vel),
        (old_far, old),
        *((syn_far.at[cut], syn.at[cut]) for cut in cuts),
        *((obs_far.at[cut], obs.at[cut]) for cut in cuts),
        (own_far, own),
        (cells_far, cells),
        (taps_far, taps),
        (off_far, off),
        (lines_far, lines),
        (line_taps_far, line_taps),
    )
    edge = jnp.zeros((wide.shape[0], PAD, lanes), jnp.float32)
    wide[:, 0:PAD, :] = edge
    wide[:, PAD + size_y :, :] = edge
    blank = jnp.zeros((REACH, size_y, lanes), jnp.float32)
    wide[0:REACH, inside, :] = blank
    wide[REACH + size_x :, inside, :] = blank
    for copy in copies[:3]:
        copy.wait()
    odd = lax.axis_index("sub") % 2
    used = 3 * REACH * size_y
    to_next[used:, :] = jnp.zeros((to_next.shape[0] - used, lanes), jnp.float32)
    half_block(Planes(to_next, size_y), (size_x - REACH) * odd, wide, vel, old)
    for copy in copies[3:]:
        copy.wait()


def send_kernel(
    devices,
    place_of,
    cap,
    block,
    wide,
    vel,
    old,
    own,
    cells,
    taps,
    off,
    lines,
    line_taps,
    syn,
    obs,
    send_far,
    to_pair,
    send,
    sems,
):
    me = lax.axis_index("sub")
    count, samples = syn.shape
    ntap = taps.shape[1]
    pack = LANES // cap
    group = LANES // EDGE
    place = iota((1, count), 1)
    owner = own[...]
    owned = same16(index16(devices, count), owner)
    one_hot = pick16(owned, jnp.ones((1, count), jnp.float32))
    chunks = [one_hot[:, at : at + LANES] for at in range(0, count, LANES)]
    ahead = index16(LANES, LANES) < across16(iota((1, LANES), 1))
    ranks = jnp.dot(
        jnp.concatenate(chunks, axis=0),
        pick16(ahead, jnp.ones((1, LANES), jnp.float32)),
        preferred_element_type=jnp.float32,
    )
    base = jnp.zeros((devices, 1), jnp.float32)
    rank = []
    for i, chunk in enumerate(chunks):
        chunk = chunk.astype(jnp.float32)
        rank.append(
            jnp.sum(
                chunk * (ranks[i * devices : (i + 1) * devices] + base), axis=0, keepdims=True
            )
        )
        base = base + jnp.sum(chunk, axis=1, keepdims=True)
    rank = jnp.concatenate(rank, axis=1).astype(jnp.int32)
    lane = index16(LANES, count)
    slot = hot16(lane, rank + (me % pack) * cap)
    edge_lane = jnp.where(
        place < SW, place, jnp.where(place >= count - SW, place - count + EDGE, -LANES)
    )
    chosen = hot16(lane, edge_lane + (me % group) * EDGE)

    row = jnp.concatenate([taps[...], jnp.zeros((1, samples - ntap), jnp.float32)], axis=1)
    starts = -(-(samples - ntap + 1) // 16) * 16
    toeplitz = pltpu.roll(
        jnp.broadcast_to(row, (starts, samples)), 0, 1, stride=1, stride_axis=0
    )
    residual = syn[...] - obs[...]
    r_high = residual.astype(jnp.bfloat16)
    r_low = (residual - r_high.astype(jnp.float32)).astype(jnp.bfloat16)
    t_high = toeplitz.astype(jnp.bfloat16)
    t_low = (toeplitz - t_high.astype(jnp.float32)).astype(jnp.bfloat16)
    all_starts = sum(
        lax.dot_general(a, b, NT_DIMS, preferred_element_type=jnp.float32)
        for a, b in ((t_high, r_low), (t_low, r_high), (t_high, r_high))
    )
    start = iota((starts, count), 0)
    offset = off[...]
    filtered = [
        jnp.sum(jnp.where(start == offset + step, all_starts, 0.0), axis=0, keepdims=True)
        for step in range(STEPS)
    ]
    both = jnp.concatenate(filtered + [jnp.zeros((8 - STEPS, count), jnp.float32)], axis=0)
    before = lines[0:1, :]
    after = lines[1:2, :]
    sources = jnp.zeros((8, count), jnp.float32)
    for reach in range(-SW, SW + 1):
        term = line_taps[0:1, reach + SW : reach + SW + 1] * (
            pltpu.roll(both, (-reach) % count, 1) if reach else both
        )
        if reach < 0:
            keep = (before >= -reach) & (place >= -reach)
        elif reach > 0:
            keep = (after >= reach) & (place < count - reach)
        else:
            keep = before >= 0
        sources = sources + jnp.where(keep, term, 0.0)
    cell = cells[...]
    high = (cell >> 8).astype(jnp.float32)
    low = (cell & 255).astype(jnp.float32)
    pieces = parts_of(sources[0:1], 3) + parts_of(sources[1:2], 3) + [high, low]
    spread = jnp.concatenate([pick16(owned, piece) for piece in pieces], axis=0)
    out = lax.dot_general(spread, slot, NT_DIMS, preferred_element_type=jnp.float32)
    part = [out[k * devices : (k + 1) * devices] for k in range(8)]
    value0 = part[0] + part[1] + part[2]
    value1 = part[3] + part[4] + part[5]
    where = 256.0 * part[6] + part[7]
    none = jnp.zeros((1, LANES), jnp.float32)

    def to_upper(rows):
        return pltpu.roll(jnp.concatenate([none, rows[:-1]], axis=0), LANES // 2, 1)

    def to_lower(rows):
        return pltpu.roll(jnp.concatenate([rows[1:], none], axis=0), LANES // 2, 1)

    def put(k, rows):
        for to, at in enumerate(place_of):
            send[at, k : k + 1, :] = rows[to : to + 1]

    put(0, value0 + to_upper(value0))
    put(1, where + to_upper(where))
    put(2, value1 + to_lower(value0))
    put(3, to_lower(where))
    count_ = jnp.where(place < SW, before, after).astype(jnp.float32)
    edge_rows = (
        parts_of(both[0:1], 3)
        + parts_of(both[1:2], 3)
        + [owner.astype(jnp.float32), high, low, count_]
    )
    edge_rows = jnp.concatenate(
        edge_rows + [jnp.zeros((16 - len(edge_rows), count), jnp.float32)], axis=0
    ).astype(jnp.bfloat16)
    edge = lax.dot_general(edge_rows, chosen, NT_DIMS, preferred_element_type=jnp.float32)
    edge_cell = edge[6:7] * float(block) + 256.0 * edge[7:8] + edge[8:9]
    shape = (devices, LANES)
    put(4, jnp.broadcast_to(edge[0:1] + edge[1:2] + edge[2:3], shape))
    put(5, jnp.broadcast_to(edge[3:4] + edge[4:5] + edge[5:6], shape))
    put(6, jnp.broadcast_to(edge_cell, shape))
    put(7, jnp.broadcast_to(edge[9:10], shape))
    sent = pltpu.make_async_copy(send, send_far, sems.at[0])
    sent.start()
    half_block(to_pair, (old.shape[0] - REACH) * (1 - me % 2), wide, vel, old)
    sent.wait()


def inner_kernel(
    old_far,
    now_far,
    vel_far,
    fwd_far,
    line_taps_far,
    partial,
    now,
    vel,
    weight0,
    weight1,
    line_taps,
    wide,
    old,
    fwd,
    sems,
):
    size_x, size_y, lanes = old.shape
    inside = slice(PAD, PAD + size_y)
    copies = started(
        sems,
        (now_far, wide.at[REACH : REACH + size_x, inside, :]),
        (vel_far, vel),
        (old_far, old),
        (fwd_far, fwd),
        (line_taps_far, line_taps),
    )
    edge = jnp.zeros((wide.shape[0], PAD, lanes), jnp.float32)
    wide[:, 0:PAD, :] = edge
    wide[:, PAD + size_y :, :] = edge
    blank = jnp.zeros((REACH, size_y, lanes), jnp.float32)
    wide[0:REACH, inside, :] = blank
    wide[REACH + size_x :, inside, :] = blank
    for copy in copies:
        copy.wait()

    for x in range(size_x):
        speed = vel[x]
        now[x] = wide[REACH + x, inside, :]
        partial[x] = (
            2.0 * now[x]
            - old[x]
            + squared(speed) * laplacian_plane(wide, x + REACH, size_y)
        )
        weight = 2.0 / (speed * speed * speed)
        f1 = fwd[1, x]
        f2 = fwd[2, x]
        weight0[x] = weight * (fwd[0, x] - 2.0 * f1 + f2)
        weight1[x] = weight * (f1 - 2.0 * f2 + fwd[3, x])


def across(field, x, low, high):
    total = None
    for k in range(1, 5):
        for at in (x - k, x + k):
            if low <= at < high:
                term = COEF[k] * field[at - low]
                total = term if total is None else total + term
    return total


def first_kernel(
    from_pair, from_next, partial, now, vel, free, scale
):
    odd = lax.axis_index("sub") % 2
    size_x = now.shape[0]
    from_next = Planes(from_next, now.shape[1])
    top = REACH + size_x

    def border(source, first_out, low):
        for i in range(REACH):
            factor = squared(source[2 * REACH + i])
            scale[first_out + i] = factor
            free[first_out + i] = source[REACH + i] + factor * across(now, low + i, 0, size_x)
        planes = range(REACH) if low < 0 else range(size_x - REACH, size_x)
        for x in planes:
            factor = squared(vel[x])
            scale[REACH + x] = factor
            free[REACH + x] = partial[x] + factor * across(source, x, low, low + REACH)

    @pl.when(odd == 0)
    def _():
        border(from_next, 0, -REACH)
        border(from_pair, top, size_x)

    @pl.when(odd == 1)
    def _():
        border(from_pair, 0, -REACH)
        border(from_next, top, size_x)


def second_kernel(
    devices,
    place_of,
    cap,
    got,
    free,
    scale,
    now,
    weight0,
    weight1,
    line_taps,
    prior_far,
    last_far,
    gradient_far,
    last,
    gradient,
    field,
    source1,
    out_sems,
):
    me = lax.axis_index("sub")
    size_x, size_y, lanes = now.shape
    rows = size_x * size_y
    halo = REACH * size_y
    block = rows * lanes
    pack = LANES // cap
    lane8 = iota((8, LANES), 1)
    shift = lanes.bit_length() - 1

    def hot_rows(cell, move, index):
        return hot16(index, (cell >> shift) + move)

    def spread(cell, values):
        at = same16(zs, cell & (lanes - 1))
        stack = []
        for value in values:
            for part in parts_of(value, 2):
                stack.append(pick16(at, part))
        return jnp.concatenate(stack, axis=0)

    def inject(a, b):
        return lax.dot_general(
            jnp.concatenate(a, axis=1),
            jnp.concatenate(b, axis=1),
            NT_DIMS,
            preferred_element_type=jnp.float32,
        )

    zs = index16(LANES, LANES)
    row_index = index16(rows, LANES)
    halo_index = index16(halo, LANES)

    own_a, own_b, low_a, low_b, high_a, high_b = [], [], [], [], [], []
    mine, other = [], []
    for g in range(devices // pack):
        tiles = [got[place_of[g * pack + q]] for q in range(pack)]
        one, two = tiles[0], tiles[pack // 2]
        for q in range(1, pack):
            later = lane8 >= q * cap
            one = jnp.where(later, tiles[q], one)
            two = jnp.where(later, tiles[(q + pack // 2) % pack], two)
        mine.append(one)
        other.append(two)
    for one in mine:
        cell = one[1:2].astype(jnp.int32)
        own_a.append(hot_rows(cell, 0, row_index))
        own_b.append(spread(cell, [one[0:1], one[2:3]]))
    for two in other:
        cell = two[1:2].astype(jnp.int32)
        low_a.append(hot_rows(cell, halo - rows, halo_index))
        low_b.append(spread(cell, [two[0:1]]))
    for two in other:
        cell = two[3:4].astype(jnp.int32)
        high_a.append(hot_rows(cell, 0, halo_index))
        high_b.append(spread(cell, [two[2:3]]))

    group = LANES // EDGE
    edge_parts = []
    for g in range(-(-devices // group)):
        total = got[place_of[g * group]]
        for i in range(g * group + 1, min(devices, (g + 1) * group)):
            total = total + got[place_of[i]]
        edge_parts.append(total)
    edge = jnp.concatenate(edge_parts, axis=1)
    width = edge.shape[1]
    spot = iota((8, width), 1)
    e = spot % EDGE
    count = edge[7:8]
    missing = jnp.zeros((8, width), jnp.float32)
    for reach in range(-SW, SW + 1):
        if reach == 0:
            continue
        if reach < 0:
            crosses = (e < -reach) & (spot >= -reach)
        else:
            crosses = (e >= EDGE - reach) & (spot < width - reach)
        keep = crosses & (count >= float(abs(reach)))
        missing = missing + jnp.where(
            keep,
            line_taps[0:1, reach + SW : reach + SW + 1] * pltpu.roll(edge, (-reach) % width, 1),
            0.0,
        )
    edge_cell = edge[6:7].astype(jnp.int32) - me * block
    edge_row = jnp.clip(edge_cell >> shift, -2 * rows, 2 * rows)
    for g in range(width // LANES):
        at = slice(g * LANES, (g + 1) * LANES)
        b = spread(edge_cell[:, at], [missing[4:5, at], missing[5:6, at]])
        own_a.append(hot16(row_index, edge_row[:, at]))
        own_b.append(b)
        low_a.append(hot16(halo_index, edge_row[:, at] + halo))
        low_b.append(b[: 2 * LANES])
        high_a.append(hot16(halo_index, edge_row[:, at] - rows))
        high_b.append(b[: 2 * LANES])

    zeros = jnp.zeros((field.shape[0], PAD, lanes), jnp.float32)
    field[:, 0:PAD, :] = zeros
    field[:, PAD + size_y :, :] = zeros
    inside = slice(PAD, PAD + size_y)
    top = REACH + size_x

    out = inject(own_a, own_b)
    low_out = inject(low_a, low_b)
    high_out = inject(high_a, high_b)
    first = (out[:, 0:lanes] + out[:, lanes : 2 * lanes]).reshape(size_x, size_y, lanes)
    source1[...] = (out[:, 2 * lanes : 3 * lanes] + out[:, 3 * lanes :]).reshape(
        size_x, size_y, lanes
    )
    field[REACH:top, inside, :] = free[REACH:top] + scale[REACH:top] * first
    done = [
        pltpu.make_async_copy(field.at[REACH:top, inside, :], prior_far, out_sems.at[0])
    ]
    done[0].start()
    first = (low_out[:, 0:lanes] + low_out[:, lanes:]).reshape(REACH, size_y, lanes)
    field[0:REACH, inside, :] = free[0:REACH] + scale[0:REACH] * first
    first = (high_out[:, 0:lanes] + high_out[:, lanes:]).reshape(REACH, size_y, lanes)
    field[top:, inside, :] = free[top:] + scale[top:] * first

    half = size_x // 2
    for part in range(2):
        planes = slice(part * half, (part + 1) * half)

        for x in range(part * half, (part + 1) * half):
            at = x + REACH
            fresh = field[at, inside, :]
            following = (
                2.0 * fresh
                - now[x]
                + scale[at] * (laplacian_plane(field, at, size_y) + source1[x])
            )
            last[x] = following
            gradient[x] = weight0[x] * fresh + weight1[x] * following

        done += started(
            out_sems.at[pl.ds(1 + 2 * part, 2)],
            (last.at[planes], last_far.at[planes]),
            (gradient.at[planes], gradient_far.at[planes]),
        )
    for copy in done:
        copy.wait()


def body(
    synthetic,
    observed,
    offsets,
    lines,
    owners,
    cells,
    taps,
    line_taps,
    velocity,
    adjoint_old,
    adjoint_now,
    forward,
):
    count = synthetic.shape[0]
    size_x, size_y, lanes = velocity.shape
    devices = lax.axis_size("sub")
    cap = max(2, 2 * count // devices)
    f32 = jnp.float32

    order = list(range(devices))[::-1]
    place_of = [order.index(i) for i in range(devices)]
    pair = [(i, i ^ 1) for i in range(devices)]
    following = [(i, i + 1) for i in range(1, devices - 1, 2)]
    following = following + [(b, a) for a, b in following]

    plane = (size_y, lanes)
    outer = size_x + 2 * REACH
    inner = pltpu.VMEM((size_x,) + plane, f32)
    padded = pltpu.VMEM((outer, size_y + 2 * PAD, lanes), f32)
    halo = pltpu.VMEM((3 * REACH,) + plane, f32)
    wider = pltpu.VMEM((outer,) + plane, f32)
    inner_far = pltpu.HBM((size_x,) + plane, f32)
    wider_far = pltpu.HBM((outer,) + plane, f32)
    dma = pltpu.SemaphoreType.DMA

    row = (1, count)
    sources = (
        adjoint_now,
        velocity,
        adjoint_old,
        owners.reshape(row),
        cells.reshape(row),
        taps.reshape(1, -1),
        offsets.reshape(row),
        lines,
        line_taps.reshape(1, -1),
        synthetic,
        observed,
    )
    fetched = (padded,) + tuple(pltpu.VMEM(a.shape, a.dtype) for a in sources[1:])
    to_next, *fetched = pl.pallas_call(
        next_kernel,
        out_shape=(pltpu.VMEM((3 * REACH * size_y + 8, lanes), f32),) + fetched,
        in_specs=[FAR] * len(sources),
        out_specs=(VMEM,) * (1 + len(sources)),
        scratch_shapes=[dma((len(sources) + 2,))],
        compiler_params=PARAMS,
        name="next",
    )(*far(*sources))
    send, to_pair = pl.pallas_call(
        functools.partial(send_kernel, devices, place_of, cap, velocity.size),
        out_shape=(pltpu.HBM((devices, 8, LANES), f32), halo),
        in_specs=[VMEM] * len(fetched),
        out_specs=(FAR, VMEM),
        scratch_shapes=[pltpu.VMEM((devices, 8, LANES), f32), dma((1,))],
        compiler_params=PARAMS,
        name="send",
    )(*(near(a) for a in fetched))
    from_next = lax.ppermute(to_next, "sub", following)
    from_pair = lax.ppermute(to_pair, "sub", pair)
    got = lax.all_to_all(
        send, "sub", split_axis=0, concat_axis=0, axis_index_groups=[order], tiled=True
    )

    partial, now, vel, weight0, weight1, line_row = pl.pallas_call(
        inner_kernel,
        out_shape=(inner,) * 5 + (pltpu.VMEM((1, line_taps.shape[0]), f32),),
        in_specs=[FAR] * 5,
        out_specs=(VMEM,) * 6,
        scratch_shapes=[padded, inner, pltpu.VMEM(forward.shape, f32), dma((5,))],
        compiler_params=PARAMS,
        name="inner",
    )(*far(adjoint_old, adjoint_now, velocity, forward, line_taps.reshape(1, -1)))
    free, scale = pl.pallas_call(
        first_kernel,
        out_shape=(wider,) * 2,
        in_specs=[VMEM] * 5,
        out_specs=(VMEM,) * 2,
        compiler_params=PARAMS,
        name="first",
    )(near(from_pair), near(from_next), near(partial), near(now), near(vel))

    field = jax.ShapeDtypeStruct((size_x,) + plane, f32)
    return pl.pallas_call(
        functools.partial(second_kernel, devices, place_of, cap),
        out_shape=(field, field, field),
        in_specs=[VMEM] * 7,
        out_specs=(FAR,) * 3,
        scratch_shapes=[
            inner,
            inner,
            pltpu.VMEM((outer, size_y + 2 * PAD, lanes), f32),
            inner,
            dma((5,)),
        ],
        compiler_params=PARAMS,
        name="second",
    )(
        near(got),
        near(free),
        near(scale),
        near(now),
        near(weight0),
        near(weight1),
        near(line_row),
    )


def solution(mesh):
    return jax.shard_map(
        body,
        mesh=mesh,
        in_specs=(
            P(("shot", "sub"), None),
            P(("shot", "sub"), None),
            P(("shot", "sub")),
            P(None, ("shot", "sub")),
            P(("shot", "sub"), None),
            P(("shot", "sub")),
            P(),
            P(),
            P("sub", None, None),
            P(("shot", "sub"), None, None),
            P(("shot", "sub"), None, None),
            P(None, ("shot", "sub"), None, None),
        ),
        out_specs=(
            P(("shot", "sub"), None, None),
            P(("shot", "sub"), None, None),
            P(("shot", "sub"), None, None),
        ),
        check_vma=False,
    )
```
